768 devices in a mesh: scene: 8 (over x, core), brick: 96 (over y, z).
Axes of the slice: x: 4, y: 8, z: 12, core: 2. Of those that a mesh axis runs over, the one named last changes fastest.
Arguments:
- features: bfloat16 [8, 49152, 64], P('scene', 'brick'), may hold values from -6 to 6
- cotangent: bfloat16 [8, 49152, 64], P('scene', 'brick'), may hold values from -6 to 6
- first_weight: bfloat16 [1728, 64], replicated, may hold values from -0.15625 to 0.15625
- second_weight: bfloat16 [1728, 64], replicated, may hold values from -0.15625 to 0.15625
- send_rows: int32 [8, 12288], P('scene', 'brick'), may hold values from 0 to 512, as said below
- gather_rows: int32 [8, 96000], P('scene', 'brick'), may hold values from 0 to 640, as said below
Outputs:
- output: bfloat16 [8, 49152, 64], P('scene', 'brick')
- grad_input: bfloat16 [8, 49152, 64], P('scene', 'brick')
- grad_first: float32 [1728, 64], replicated
- grad_second: float32 [1728, 64], replicated
The draws below stay inside these ranges and needn't reach their ends.
Inputs may be any that keep to these rules, and one draw needn't show every extreme that they name: `send_rows`: entries equal to 512 are empty slots; used entries come first in each half and name voxels on the face of active bricks towards that neighbour; in every draw some pair of neighbouring indices sends all 64 rows to each other. Index 0 sends nothing down, the last index nothing up. `gather_rows`: row 640 is the zero row; inactive slots read only it; rows 512 and up read boundary rows in the order of the neighbour's send list. Every index of brick holds exactly one active brick slot, and bricks touch only bricks of the same or an adjacent index.
All inputs are finite; a program needn't handle non-finite values.
Results may differ from the reference program's by a relative error of at most 0.0059.
Values may be sent and summed in bfloat16 or wider, within the bound.
A program may use at most 32 MiB of HBM per device.

```python
import jax
import jax.numpy as jnp
from jax import lax

C = 64
EDGE = 8
B_CAP = 1
SIDE_Z = 2
VOX = 512
CAPV = 64
POOL = 641
PADDED = 1000
ROWS = 49152
N_SCENE = 8
N_BRICK = 96


def scene_tables(key):
    base = jax.random.fold_in(key, 1234)
    count_key, order_key, pair_key = jax.random.split(base, 3)
    scenes = N_SCENE
    devices = N_BRICK
    slots = B_CAP
    edge = EDGE
    side_y = 2
    places = side_y * SIDE_Z
    counts = jax.random.randint(count_key, (scenes, devices), (slots + 1) // 2, slots + 1)
    pair = jax.random.randint(pair_key, (scenes,), 0, devices - 1)
    device_ids = jnp.arange(devices)
    forced = (device_ids[None, :] == pair[:, None]) | (device_ids[None, :] == pair[:, None] + 1)
    counts = jnp.where(forced, slots, counts)
    scores = jax.random.randint(order_key, (scenes, devices, places), 0, 1 << 20) * places + jnp.arange(places)
    orders = jnp.argsort(scores, axis=-1).astype(jnp.int32)
    source = jnp.where(device_ids[None, :] == pair[:, None] + 1, pair[:, None], device_ids[None, :])
    orders = jnp.take_along_axis(orders, jnp.broadcast_to(source[:, :, None], (scenes, devices, places)), axis=1)
    position = orders[:, :, :slots]
    slot_ids = jnp.arange(slots)
    active = slot_ids[None, None, :] < counts[:, :, None]
    match = (position[..., None] == jnp.arange(places)) & active[..., None]
    slot_map = jnp.sum(jnp.where(match, slot_ids[None, None, :, None] + 1, 0), axis=2) - 1
    occupied = slot_map >= 0
    none_row = jnp.zeros((scenes, 1, places), bool)
    occupied_up = jnp.concatenate([occupied[:, 1:], none_row], axis=1)
    occupied_down = jnp.concatenate([none_row, occupied[:, :-1]], axis=1)
    pos_y = position // SIDE_Z
    pos_z = position % SIDE_Z
    place_y = jnp.arange(places) // SIDE_Z
    place_z = jnp.arange(places) % SIDE_Z
    inner = jnp.arange(edge)
    glob_y = pos_y[..., None] * edge + inner
    glob_z = pos_z[..., None] * edge + inner
    reach_y = (glob_y[..., None] >= place_y * edge - 1) & (glob_y[..., None] <= place_y * edge + edge)
    reach_z = (glob_z[..., None] >= place_z * edge - 1) & (glob_z[..., None] <= place_z * edge + edge)

    def side(occ_near, face):
        wanted = jnp.any(reach_y[:, :, :, :, None, :] & reach_z[:, :, :, None, :, :] & occ_near[:, :, None, None, None, :], axis=-1)
        wanted = wanted & active[:, :, :, None, None]
        flags = wanted.reshape(scenes, devices, CAPV).astype(jnp.int32)
        ranks = jnp.cumsum(flags, axis=-1) - 1
        candidate = (slot_ids[:, None, None] * edge ** 3 + face * edge * edge + inner[None, :, None] * edge + inner[None, None, :]).reshape(CAPV)
        order = jnp.argsort((1 - flags) * CAPV + jnp.arange(CAPV), axis=-1)
        chosen = candidate[order]
        used = jnp.arange(CAPV) < jnp.sum(flags, axis=-1, keepdims=True)
        return (jnp.where(used, chosen, VOX), ranks)
    rows_down, rank_down = side(occupied_down, 0)
    rows_up, rank_up = side(occupied_up, edge - 1)
    send = jnp.concatenate([rows_down, rows_up], axis=-1).reshape(scenes, devices * 2 * CAPV).astype(jnp.int32)
    span = jnp.arange(edge + 2)
    offset = jnp.where(span == 0, -1, jnp.where(span == edge + 1, 1, 0))
    within = span - 1 - offset * edge
    near_y = pos_y[..., None] + offset
    near_z = pos_z[..., None] + offset
    inside = ((near_y >= 0) & (near_y < side_y))[..., :, None] & ((near_z >= 0) & (near_z < SIDE_Z))[..., None, :]
    near_place = jnp.clip(near_y, 0, side_y - 1)[..., :, None] * SIDE_Z + jnp.clip(near_z, 0, SIDE_Z - 1)[..., None, :]
    flat_place = near_place.reshape(scenes, devices, -1)

    def lookup(map_near):
        return jnp.take_along_axis(map_near, flat_place, axis=2).reshape(near_place.shape)
    none_map = jnp.full((scenes, 1, places), -1, slot_map.dtype)
    map_up = jnp.concatenate([slot_map[:, 1:], none_map], axis=1)
    map_down = jnp.concatenate([none_map, slot_map[:, :-1]], axis=1)
    here = lookup(slot_map)
    above = lookup(map_up)
    below = lookup(map_down)
    face_index = within[:, None] * edge + within[None, :]
    zero_ranks = jnp.zeros((scenes, 1, CAPV), rank_down.dtype)
    ranks_above = jnp.concatenate([rank_down[:, 1:], zero_ranks], axis=1)
    ranks_below = jnp.concatenate([zero_ranks, rank_up[:, :-1]], axis=1)

    def rank_at(ranks_near, slot_near):
        index = jnp.maximum(slot_near, 0) * edge * edge + face_index
        return jnp.take_along_axis(ranks_near, index.reshape(scenes, devices, -1), axis=2).reshape(slot_near.shape)
    zero_row = POOL - 1
    from_above = jnp.where(inside & (above >= 0), VOX + CAPV + rank_at(ranks_above, above), zero_row)
    from_below = jnp.where(inside & (below >= 0), VOX + rank_at(ranks_below, below), zero_row)
    local_rows = jnp.maximum(here, 0)[:, :, :, None, :, :] * edge ** 3 + within[None, None, None, :, None, None] * edge * edge + face_index[None, None, None, None, :, :]
    pick_local = jnp.where((inside & (here >= 0))[:, :, :, None, :, :], local_rows, zero_row)
    step_x = offset[None, None, None, :, None, None]
    rows_all = jnp.where(step_x == 0, pick_local, jnp.where(step_x > 0, from_above[:, :, :, None, :, :], from_below[:, :, :, None, :, :]))
    rows_all = jnp.where(active[:, :, :, None, None, None], rows_all, zero_row)
    gather = rows_all.reshape(scenes, devices * slots * (edge + 2) ** 3).astype(jnp.int32)
    return (send, gather)


def draw_send_rows(key, part):
    return scene_tables(key)[0]


def draw_gather_rows(key, part):
    return scene_tables(key)[1]


def shard_levels(stream_key, extent, cuts, low, high):
    level, own = 1.0, jax.random.fold_in(stream_key, 6)
    for dim, parts in cuts:
        heights = jnp.exp(jax.random.uniform(jax.random.fold_in(own, dim), (parts,), jnp.float32, low / len(cuts), high / len(cuts)))
        level = level * jnp.repeat(heights, extent[dim] // parts).reshape([-1 if axis == dim else 1 for axis in range(len(extent))])
    return level


def centred(rng, shape, width, most, cuts=(), held_as=jnp.bfloat16):
    values = jax.random.normal(rng, shape, jnp.float32) * width
    if len(cuts) > 0:
        values = shard_levels(rng, shape, cuts, -0.22, 0.18) * values
    return jnp.clip(values, min=-most, max=most).astype(held_as)


def setup_inputs(seed: int = 0) -> dict:
    splits = jax.random.split(jax.random.key(seed), 7)
    return {
        "features": centred(splits[0], (N_SCENE, ROWS, C), 1.0, 6.0, ((0, 8), (1, 96))),
        "cotangent": centred(splits[1], (N_SCENE, ROWS, C), 1.0, 6.0, ((0, 8), (1, 96))),
        "first_weight": centred(splits[2], (27 * C, C), (27 * C) ** -0.5, 0.15625),
        "second_weight": centred(splits[3], (27 * C, C), (27 * C) ** -0.5, 0.15625),
        "send_rows": draw_send_rows(jax.random.fold_in(splits[6], 71), 0),
        "gather_rows": draw_gather_rows(jax.random.fold_in(splits[6], 71), 0),
    }


def silu_slope(values):
    sig = jax.nn.sigmoid(values)
    return sig * (1.0 + values * (1.0 - sig))


def scene_padded(values, send_list, gather_list):
    blocks = values.reshape(N_BRICK, VOX, C)
    zero_rows = jnp.zeros((N_BRICK, 1, C), values.dtype)
    extended = jnp.concatenate([blocks, zero_rows], axis=1)
    sent = jax.vmap(lambda rows, index: jnp.take(rows, index, axis=0))(extended, send_list.reshape(N_BRICK, 2 * CAPV))
    empty = jnp.zeros((1, CAPV, C), values.dtype)
    from_lower = jnp.concatenate([empty, sent[:-1, CAPV:]], axis=0)
    from_upper = jnp.concatenate([sent[1:, :CAPV], empty], axis=0)
    pool = jnp.concatenate([blocks, from_lower, from_upper, zero_rows], axis=1)
    padded = jax.vmap(lambda rows, index: jnp.take(rows, index, axis=0))(pool, gather_list.reshape(N_BRICK, B_CAP * PADDED))
    return padded.reshape(N_BRICK * B_CAP, EDGE + 2, EDGE + 2, EDGE + 2, C)


def window_rows(padded, row_off, col_off):
    slabs = [padded[:, row_off:row_off + EDGE, col_off:col_off + EDGE, depth:depth + EDGE, :] for depth in range(3)]
    return jnp.concatenate(slabs, axis=-1).reshape(-1, 3 * C)


def convolve(padded, weight):
    accumulated = jnp.zeros((padded.shape[0] * EDGE ** 3, weight.shape[1]), jnp.float32)
    for row_off in range(3):
        for col_off in range(3):
            start = (row_off * 3 + col_off) * 3 * C
            accumulated = accumulated + jnp.dot(window_rows(padded, row_off, col_off), weight[start:start + 3 * C], preferred_element_type=jnp.float32)
    return accumulated


def weight_gradient(padded, delta_rows):
    pieces = []
    for row_off in range(3):
        for col_off in range(3):
            pieces.append(lax.dot_general(window_rows(padded, row_off, col_off), delta_rows, (((0,), (0,)), ((), ())), preferred_element_type=jnp.float32))
    return jnp.concatenate(pieces, axis=0)


def flipped(weight):
    return jnp.transpose(weight.reshape(27, C, C)[::-1], (0, 2, 1)).reshape(27 * C, C)


def one_scene(items):
    values, cot_rows, send_list, gather_list, first_weight, second_weight = items
    padded_input = scene_padded(values, send_list, gather_list)
    first_pre = convolve(padded_input, first_weight)
    first_act = (first_pre * jax.nn.sigmoid(first_pre)).astype(jnp.bfloat16)
    padded_act = scene_padded(first_act, send_list, gather_list)
    second_pre = convolve(padded_act, second_weight)
    output = (second_pre * jax.nn.sigmoid(second_pre)).astype(jnp.bfloat16)
    second_delta = (cot_rows.astype(jnp.float32) * silu_slope(second_pre)).astype(jnp.bfloat16)
    grad_second = weight_gradient(padded_act, second_delta)
    first_back = convolve(scene_padded(second_delta, send_list, gather_list), flipped(second_weight))
    first_delta = (first_back * silu_slope(first_pre)).astype(jnp.bfloat16)
    grad_first = weight_gradient(padded_input, first_delta)
    grad_input = convolve(scene_padded(first_delta, send_list, gather_list), flipped(first_weight)).astype(jnp.bfloat16)
    return output, grad_input, grad_first, grad_second


def reference(features, cotangent, first_weight, second_weight, send_rows, gather_rows):
    def step(items):
        return one_scene((items[0], items[1], items[2], items[3], first_weight, second_weight))

    output, grad_input, grad_first, grad_second = lax.map(step, (features, cotangent, send_rows, gather_rows))
    factor = float(N_SCENE * N_BRICK * VOX) ** -0.5
    return output, grad_input, jnp.sum(grad_first, axis=0) * factor, jnp.sum(grad_second, axis=0) * factor
```

```python
import functools

import jax
import jax.numpy as jnp
from jax import lax
from jax.experimental import pallas as pl
from jax.experimental.pallas import tpu as pltpu
from jax.sharding import PartitionSpec as P

EDGE = 8
VOX = 512
C = 64
TAPS = 27
LANES = 128
MESH = pl.DeviceIdType.MESH
BLOCKS = 14


def extended(block, sides, width):
    for axis, dim in sides:
        count = lax.axis_size(axis)
        forward = [(i, i + 1) for i in range(count - 1)]
        backward = [(target, source) for source, target in forward]
        low = lax.ppermute(
            lax.slice_in_dim(block, block.shape[dim] - width, None, axis=dim), axis, forward
        )
        high = lax.ppermute(lax.slice_in_dim(block, 0, width, axis=dim), axis, backward)
        block = jnp.concatenate([low, block, high], axis=dim)
    return block


def silu_slope(values):
    sig = jax.nn.sigmoid(values)
    return sig * (1.0 + values * (1.0 - sig))


def outgoing_rows(values, send_list):
    zero_row = jnp.zeros((1, values.shape[1]), values.dtype)
    return jnp.take(jnp.concatenate([values, zero_row], axis=0), send_list, axis=0)


def assemble(values, arrived, gather_list, slot_width):
    zero_row = jnp.zeros((1, values.shape[1]), values.dtype)
    pool = jnp.concatenate(
        [values, arrived[:slot_width], arrived[3 * slot_width :], zero_row], axis=0
    )
    return jnp.take(pool, gather_list, axis=0).reshape(
        -1, EDGE + 2, EDGE + 2, EDGE + 2, values.shape[1]
    )


def window_rows(padded, row_off, col_off, extent):
    slabs = [
        padded[:, row_off : row_off + extent, col_off : col_off + extent, depth : depth + extent, :]
        for depth in range(3)
    ]
    return jnp.concatenate(slabs, axis=-1).reshape(-1, 3 * padded.shape[-1])


def convolve(padded, weight, extent):
    width = padded.shape[-1]
    accumulated = jnp.zeros((padded.shape[0] * extent**3, weight.shape[1]), jnp.float32)
    for row_off in range(3):
        for col_off in range(3):
            start = (row_off * 3 + col_off) * 3 * width
            accumulated = accumulated + jnp.dot(
                window_rows(padded, row_off, col_off, extent),
                weight[start : start + 3 * width],
                preferred_element_type=jnp.float32,
            )
    return accumulated


def weight_gradient(padded, delta_rows):
    pieces = []
    for row_off in range(3):
        for col_off in range(3):
            pieces.append(
                lax.dot_general(
                    delta_rows,
                    window_rows(padded, row_off, col_off, EDGE),
                    (((0,), (0,)), ((), ())),
                    preferred_element_type=jnp.float32,
                )
            )
    wide = jnp.concatenate(pieces, axis=1)
    wide = jnp.pad(wide, ((0, 0), (0, BLOCKS * LANES - wide.shape[1])))
    return jnp.concatenate(jnp.split(wide, BLOCKS, axis=1), axis=0)


def flipped(weight):
    width = weight.shape[1]
    return jnp.transpose(weight.reshape(27, width, width)[::-1], (0, 2, 1)).reshape(
        27 * width, width
    )


def brick_grid(count):
    for rows in (8, 4, 2):
        if count % rows == 0 and count // rows > 1:
            return rows, count // rows
    return 1, count


class Position:
    def __init__(self, scenes, bricks):
        self.scenes = scenes
        self.bricks = bricks
        self.rows, self.cols = brick_grid(bricks)
        self.scene = lax.axis_index("scene")
        self.brick = lax.axis_index("brick")
        self.row = self.brick // self.cols
        self.col = lax.rem(self.brick, self.cols)

    def scene_peer(self, step):
        return lax.rem(self.scene + step, self.scenes)

    def row_peer(self, step):
        return lax.rem(self.row + step, self.rows)

    def col_peer(self, step):
        return lax.rem(self.col + step, self.cols)

    def scene_id(self, step):
        return (self.scene_peer(step), self.brick)

    def row_id(self, step):
        return (self.scene, self.row_peer(step) * self.cols + self.col)

    def col_id(self, step):
        return (self.scene, self.row * self.cols + self.col_peer(step))

    def reduce_peers(self):
        peers = [self.scene_id(k) for k in range(1, self.scenes)]
        peers += [self.row_id(k) for k in range(1, self.rows)]
        peers += [self.col_id(k) for k in range(1, self.cols)]
        return peers


def meet(peers):
    barrier = pltpu.get_barrier_semaphore()
    for peer in peers:
        pl.semaphore_signal(barrier, inc=1, device_id=peer, device_id_type=MESH)
    pl.semaphore_wait(barrier, len(peers))


def remote(src, dst, send_sem, recv_sem, peer):
    copy = pltpu.make_async_remote_copy(
        src_ref=src, dst_ref=dst, send_sem=send_sem, recv_sem=recv_sem,
        device_id=peer, device_id_type=MESH,
    )
    copy.start()
    return copy


class Reduction:
    def __init__(self, pos, refs):
        self.pos = pos
        (self.send_scene, self.recv_scene, self.send_row, self.recv_row,
         self.slots, self.full, *sems) = refs
        self.sems = [(sems[2 * i], sems[2 * i + 1]) for i in range(5)]
        self.started = []

    @staticmethod
    def scratch(scenes, rows, cols):
        piece = 1024 // scenes
        small = piece // rows
        counts = (scenes, rows, cols, rows, scenes)
        sems = []
        for count in counts:
            sems += [pltpu.SemaphoreType.DMA((count - 1,))] * 2
        return [
            pltpu.VMEM((scenes, piece, LANES), jnp.bfloat16),
            pltpu.VMEM((scenes - 1, piece, LANES), jnp.bfloat16),
            pltpu.VMEM((rows, small, LANES), jnp.bfloat16),
            pltpu.VMEM((rows - 1, small, LANES), jnp.bfloat16),
            pltpu.VMEM((cols, small, LANES), jnp.bfloat16),
            pltpu.VMEM((scenes, rows, small, LANES), jnp.bfloat16),
        ] + sems

    def put(self, block, values):
        piece = self.send_scene.shape[1]
        rows = values.shape[0]
        start = block * rows
        for at in range(start, start + rows, min(rows, piece)):
            count = min(rows, piece)
            self.send_scene[at // piece, pl.ds(at % piece, count), :] = values[
                at - start : at - start + count
            ]

    def send(self, which, src, dst, peers):
        self.current = []
        for k, (peer, s, d) in enumerate(zip(peers, src, dst)):
            sems = self.sems[which]
            self.current.append(remote(s, d, sems[0].at[k], sems[1].at[k], peer))
        self.started += self.current

    def arrive(self):
        for copy in self.current:
            copy.wait_recv()

    def start_scene(self):
        pos = self.pos
        n = pos.scenes
        self.send(0, [self.send_scene.at[pos.scene_peer(k)] for k in range(1, n)],
                  [self.recv_scene.at[k - 1] for k in range(1, n)],
                  [pos.scene_id(k) for k in range(1, n)])

    def start_row(self):
        self.arrive()
        pos = self.pos
        n = pos.rows
        total = self.send_scene[pos.scene].astype(jnp.float32)
        for k in range(pos.scenes - 1):
            total = total + self.recv_scene[k].astype(jnp.float32)
        self.send_row[...] = total.astype(jnp.bfloat16).reshape(self.send_row.shape)
        self.send(1, [self.send_row.at[pos.row_peer(k)] for k in range(1, n)],
                  [self.recv_row.at[k - 1] for k in range(1, n)],
                  [pos.row_id(k) for k in range(1, n)])

    def start_col(self):
        self.arrive()
        pos = self.pos
        n = pos.cols
        total = self.send_row[pos.row].astype(jnp.float32)
        for k in range(pos.rows - 1):
            total = total + self.recv_row[k].astype(jnp.float32)
        self.slots[pos.col] = total.astype(jnp.bfloat16)
        own = self.slots.at[pos.col]
        self.send(2, [own] * (n - 1), [own] * (n - 1), [pos.col_id(k) for k in range(1, n)])

    def start_row_back(self):
        self.arrive()
        pos = self.pos
        n = pos.rows
        total = self.slots[0].astype(jnp.float32)
        for k in range(1, pos.cols):
            total = total + self.slots[k].astype(jnp.float32)
        self.full[pos.scene, pos.row] = total.astype(jnp.bfloat16)
        own = self.full.at[pos.scene, pos.row]
        self.send(3, [own] * (n - 1), [own] * (n - 1), [pos.row_id(k) for k in range(1, n)])

    def start_scene_back(self):
        self.arrive()
        pos = self.pos
        n = pos.scenes
        own = self.full.at[pos.scene]
        self.send(4, [own] * (n - 1), [own] * (n - 1), [pos.scene_id(k) for k in range(1, n)])

    def finish(self, out, scale):
        self.arrive()
        everything = self.full[...].reshape(1024, LANES)
        for block in range(BLOCKS):
            rows = min(LANES, TAPS * C - block * LANES)
            piece = everything[block * C : (block + 1) * C].astype(jnp.float32) * scale
            out[pl.ds(block * LANES, rows), :] = jnp.transpose(piece)[:rows]
        for copy in self.started:
            copy.wait_send()


def reduce_kernel(scenes, bricks, first, second, out_first, out_second, *scratch):
    pos = Position(scenes, bricks)
    meet(pos.reduce_peers())
    half = len(scratch) // 2
    sums = [Reduction(pos, scratch[:half]), Reduction(pos, scratch[half:])]
    scale = float(scenes * bricks * VOX) ** (-0.5)
    for one, source in zip(sums, (first, second)):
        for block in range(BLOCKS):
            one.put(block, source[pl.ds(block * C, C), :].astype(jnp.bfloat16))
        for block in (BLOCKS, BLOCKS + 1):
            one.put(block, jnp.zeros((C, LANES), jnp.bfloat16))
        one.start_scene()
    for step in ("start_row", "start_col", "start_row_back", "start_scene_back"):
        for one in sums:
            getattr(one, step)()
    for one, out in zip(sums, (out_first, out_second)):
        one.finish(out, scale)


def reduce_all(first, second):
    scenes, bricks = lax.axis_size("scene"), lax.axis_size("brick")
    rows, cols = brick_grid(bricks)
    shape = jax.ShapeDtypeStruct((TAPS * C, C), jnp.float32)
    return pl.pallas_call(
        functools.partial(reduce_kernel, scenes, bricks),
        out_shape=(shape, shape),
        in_specs=[pl.BlockSpec(memory_space=pltpu.VMEM)] * 2,
        out_specs=[pl.BlockSpec(memory_space=pltpu.VMEM)] * 2,
        scratch_shapes=Reduction.scratch(scenes, rows, cols) * 2,
        compiler_params=pltpu.CompilerParams(
            collective_id=0, has_side_effects=True, vmem_limit_bytes=48 * 1024 * 1024
        ),
    )(first, second)


def shards(features, cotangent, first_weight, second_weight, send_rows, gather_rows):
    local_feat = features[0]
    local_cot = cotangent[0]
    send_list = send_rows[0]
    gather_list = gather_rows[0]
    slot_width = send_list.shape[0] // 2

    def forward_pad(values):
        arrived = extended(outgoing_rows(values, send_list), (("brick", 0),), slot_width)
        return assemble(values, arrived, gather_list, slot_width)

    padded_input = forward_pad(local_feat)
    first_pre = convolve(padded_input, first_weight, EDGE)
    first_act = (first_pre * jax.nn.sigmoid(first_pre)).astype(jnp.bfloat16)
    padded_act = forward_pad(first_act)
    second_pre = convolve(padded_act, second_weight, EDGE)
    output = (second_pre * jax.nn.sigmoid(second_pre)).astype(jnp.bfloat16)
    second_delta = (local_cot.astype(jnp.float32) * silu_slope(second_pre)).astype(jnp.bfloat16)
    grad_second = weight_gradient(padded_act, second_delta)
    first_back = convolve(forward_pad(second_delta), flipped(second_weight), EDGE)
    first_delta = (first_back * silu_slope(first_pre)).astype(jnp.bfloat16)
    grad_first = weight_gradient(padded_input, first_delta)
    input_back = convolve(forward_pad(first_delta), flipped(first_weight), EDGE)
    grad_input = input_back.astype(jnp.bfloat16)
    grad_first, grad_second = reduce_all(grad_first, grad_second)
    return (output[None], grad_input[None], grad_first, grad_second)


def solution(mesh):
    in_specs = (
        P("scene", "brick", None),
        P("scene", "brick", None),
        P(),
        P(),
        P("scene", "brick"),
        P("scene", "brick"),
    )
    out_specs = (P("scene", "brick", None), P("scene", "brick", None), P(), P())
    return jax.shard_map(shards, mesh=mesh, in_specs=in_specs, out_specs=out_specs, check_vma=False)
```

```python
import functools

import jax
import jax.numpy as jnp
from jax import lax
from jax.experimental import pallas as pl
from jax.experimental.pallas import tpu as pltpu
from jax.sharding import PartitionSpec as P

EDGE = 8
VOX = 512
C = 64
TAPS = 27
LANES = 128
MESH = pl.DeviceIdType.MESH
BLOCKS = 14
SPAN = EDGE + 2
CELLS = SPAN**3
SLAB = SPAN * SPAN * EDGE
POOL = VOX + LANES
PAIRS = 9
DEEP = 256
EXCHANGES = 4


def brick_grid(count):
    for rows in (8, 4, 2):
        if count % rows == 0 and count // rows > 1:
            return rows, count // rows
    return 1, count


class Position:
    def __init__(self, scenes, bricks):
        self.scenes = scenes
        self.bricks = bricks
        self.rows, self.cols = brick_grid(bricks)
        self.scene = lax.axis_index("scene")
        self.brick = lax.axis_index("brick")
        self.row = self.brick // self.cols
        self.col = lax.rem(self.brick, self.cols)

    def scene_peer(self, step):
        return lax.rem(self.scene + step, self.scenes)

    def row_peer(self, step):
        return lax.rem(self.row + step, self.rows)

    def col_peer(self, step):
        return lax.rem(self.col + step, self.cols)

    def scene_id(self, step):
        return (self.scene_peer(step), self.brick)

    def row_id(self, step):
        return (self.scene, self.row_peer(step) * self.cols + self.col)

    def col_id(self, step):
        return (self.scene, self.row * self.cols + self.col_peer(step))

    def down_id(self):
        return (self.scene, lax.rem(self.brick + self.bricks - 1, self.bricks))

    def up_id(self):
        return (self.scene, lax.rem(self.brick + 1, self.bricks))

    def reduce_peers(self):
        peers = [self.scene_id(k) for k in range(1, self.scenes)]
        peers += [self.row_id(k) for k in range(1, self.rows)]
        peers += [self.col_id(k) for k in range(1, self.cols)]
        return peers


def greet(peers):
    barrier = pltpu.get_barrier_semaphore()
    for peer in peers:
        pl.semaphore_signal(barrier, inc=1, device_id=peer, device_id_type=MESH)


def await_peers(peers):
    pl.semaphore_wait(pltpu.get_barrier_semaphore(), len(peers))


def remote(src, dst, send_sem, recv_sem, peer):
    copy = pltpu.make_async_remote_copy(
        src_ref=src, dst_ref=dst, send_sem=send_sem, recv_sem=recv_sem,
        device_id=peer, device_id_type=MESH,
    )
    copy.start()
    return copy


class Reduction:
    def __init__(self, pos, refs):
        self.pos = pos
        (self.send_scene, self.recv_scene, self.send_row, self.recv_row,
         self.slots, self.full, *sems) = refs
        self.sems = [(sems[2 * i], sems[2 * i + 1]) for i in range(5)]
        self.started = []

    @staticmethod
    def scratch(scenes, rows, cols):
        piece = 1024 // scenes
        small = piece // rows
        counts = (scenes, rows, cols, rows, scenes)
        sems = []
        for count in counts:
            sems += [pltpu.SemaphoreType.DMA((count - 1,))] * 2
        return [
            pltpu.VMEM((scenes, piece, LANES), jnp.bfloat16),
            pltpu.VMEM((scenes - 1, piece, LANES), jnp.bfloat16),
            pltpu.VMEM((rows, small, LANES), jnp.bfloat16),
            pltpu.VMEM((rows - 1, small, LANES), jnp.bfloat16),
            pltpu.VMEM((cols, small, LANES), jnp.bfloat16),
            pltpu.VMEM((scenes, rows, small, LANES), jnp.bfloat16),
        ] + sems

    def put(self, block, values):
        piece = self.send_scene.shape[1]
        rows = values.shape[0]
        start = block * rows
        for at in range(start, start + rows, min(rows, piece)):
            count = min(rows, piece)
            self.send_scene[at // piece, pl.ds(at % piece, count), :] = values[
                at - start : at - start + count
            ]

    def send(self, which, src, dst, peers):
        self.current = []
        for k, (peer, s, d) in enumerate(zip(peers, src, dst)):
            sems = self.sems[which]
            self.current.append(remote(s, d, sems[0].at[k], sems[1].at[k], peer))
        self.started += self.current

    def arrive(self):
        for copy in self.current:
            copy.wait_recv()

    def start_scene(self):
        pos = self.pos
        n = pos.scenes
        self.send(0, [self.send_scene.at[pos.scene_peer(k)] for k in range(1, n)],
                  [self.recv_scene.at[k - 1] for k in range(1, n)],
                  [pos.scene_id(k) for k in range(1, n)])

    def start_row(self):
        self.arrive()
        pos = self.pos
        n = pos.rows
        total = self.send_scene[pos.scene].astype(jnp.float32)
        for k in range(pos.scenes - 1):
            total = total + self.recv_scene[k].astype(jnp.float32)
        self.send_row[...] = total.astype(jnp.bfloat16).reshape(self.send_row.shape)
        self.send(1, [self.send_row.at[pos.row_peer(k)] for k in range(1, n)],
                  [self.recv_row.at[k - 1] for k in range(1, n)],
                  [pos.row_id(k) for k in range(1, n)])

    def start_col(self):
        self.arrive()
        pos = self.pos
        n = pos.cols
        total = self.send_row[pos.row].astype(jnp.float32)
        for k in range(pos.rows - 1):
            total = total + self.recv_row[k].astype(jnp.float32)
        self.slots[pos.col] = total.astype(jnp.bfloat16)
        own = self.slots.at[pos.col]
        self.send(2, [own] * (n - 1), [own] * (n - 1), [pos.col_id(k) for k in range(1, n)])

    def start_row_back(self):
        self.arrive()
        pos = self.pos
        n = pos.rows
        total = self.slots[0].astype(jnp.float32)
        for k in range(1, pos.cols):
            total = total + self.slots[k].astype(jnp.float32)
        self.full[pos.scene, pos.row] = total.astype(jnp.bfloat16)
        own = self.full.at[pos.scene, pos.row]
        self.send(3, [own] * (n - 1), [own] * (n - 1), [pos.row_id(k) for k in range(1, n)])

    def start_scene_back(self):
        self.arrive()
        pos = self.pos
        n = pos.scenes
        own = self.full.at[pos.scene]
        self.send(4, [own] * (n - 1), [own] * (n - 1), [pos.scene_id(k) for k in range(1, n)])

    def finish(self, out, scale):
        self.arrive()
        everything = self.full[...].reshape(1024, LANES)
        for block in range(BLOCKS):
            piece = everything[block * C : (block + 1) * C].astype(jnp.float32) * scale
            piece = jnp.transpose(piece)
            if block < PAIRS:
                out[pl.ds(block * 3 * C, 2 * C), :] = piece
            else:
                for half in range(2):
                    pair = 2 * (block - PAIRS) + half
                    if pair < PAIRS:
                        out[pl.ds(pair * 3 * C + 2 * C, C), :] = piece[half * C : (half + 1) * C]
        for copy in self.started:
            copy.wait_send()


def hot(columns, width):
    lane = lax.broadcasted_iota(jnp.int32, (1, LANES), 1).astype(jnp.float32)
    parts = [
        jnp.where(columns == lane + float(at), 1.0, 0.0).astype(jnp.bfloat16)
        for at in range(0, width, LANES)
    ]
    return jnp.concatenate(parts, axis=1)


def as_columns(row):
    return jnp.transpose(jnp.broadcast_to(row, (LANES, LANES)))


def twice(values):
    return jnp.concatenate([values, values], axis=1)


def matmul(left, right):
    return jnp.dot(left, right, preferred_element_type=jnp.float32)


class Field:
    def __init__(self, even, odd):
        self.even = even
        self.odd = odd

    def window(self, pair):
        a, b = pair // 3, pair % 3
        if b == 1:
            rows = self.odd[a : a + EDGE]
        else:
            rows = self.even[a : a + EDGE, EDGE * b : EDGE * b + VOX // EDGE]
        return rows.reshape(VOX, DEEP)

    def fill(self, pads):
        low = lax.broadcasted_iota(jnp.int32, (1, LANES), 1) < C
        first = jnp.where(low, pads[0][...], pads[1][...]).reshape(SPAN, SPAN * EDGE, LANES)
        last = pads[2][...].reshape(SPAN, SPAN * EDGE, LANES)
        odd = slice(EDGE, EDGE + VOX // EDGE)
        for at, part in ((0, first), (LANES, last)):
            self.even[:, :, at : at + LANES] = part.astype(jnp.bfloat16)
            self.odd[:, :, at : at + LANES] = part[:, odd].astype(jnp.bfloat16)

    def conv(self, weight):
        total = matmul(self.window(0), weight[0])
        for pair in range(1, PAIRS):
            total = total + matmul(self.window(pair), weight[pair])
        return total


def weight_gradient(field, delta, put):
    low = lax.broadcasted_iota(jnp.int32, (1, LANES), 1) < C
    turned = jnp.transpose(delta[:, :C]).astype(jnp.bfloat16)
    held = None
    for pair in range(PAIRS):
        got = matmul(turned, field.window(pair))
        put(pair, got[:, :LANES].astype(jnp.bfloat16))
        last = got[:, LANES:]
        if pair % 2 == 0:
            held = last
        else:
            put(PAIRS + pair // 2, jnp.where(low, held, last).astype(jnp.bfloat16))
    put(PAIRS + PAIRS // 2, held.astype(jnp.bfloat16))


def spread_weight(weight, plain, flip):
    zero = jnp.zeros((C, LANES), jnp.bfloat16)
    for pair in range(PAIRS):
        plain[pair, : 3 * C, :] = twice(weight[pl.ds(pair * 3 * C, 3 * C), :])
        plain[pair, 3 * C :, :] = zero
        flip[pair, 3 * C :, :] = zero
        for c in range(3):
            source = (TAPS - 1 - (3 * pair + c)) * C
            block = twice(weight[pl.ds(source, C), :].astype(jnp.float32))
            block = jnp.transpose(block)[:C]
            block = twice(block)
            flip[pair, c * C : (c + 1) * C, :] = block.astype(jnp.bfloat16)


def step_kernel(
    scenes, bricks, features, cotangent, first_weight, second_weight, send_rows, gather_rows,
    output, grad_input, grad_first, grad_second,
    indices, columns, gather_hot, send_hot, pads, halo_out, halo_in, halo_send, halo_recv,
    first_plain, first_flip, second_plain, second_flip,
    even_in, odd_in, even_act, odd_act, even_delta, odd_delta, first_pre_ref, *reduction,
):
    pos = Position(scenes, bricks)
    peers = [pos.down_id(), pos.up_id()] + pos.reduce_peers()
    greet(peers)
    half = len(reduction) // 2
    first_sum = Reduction(pos, reduction[:half])
    second_sum = Reduction(pos, reduction[half:])
    halos = []

    def send_halo(values):
        at = len(halos)
        halo_out[at] = matmul(send_hot[...], values).astype(jnp.bfloat16)
        if at == 0:
            await_peers(peers)
        halos.append([
            remote(halo_out.at[at, pl.ds(64 * way, 64)], halo_in.at[at, pl.ds(64 * (1 - way), 64)],
                   halo_send.at[at, way], halo_recv.at[at, way], peer)
            for way, peer in enumerate((pos.down_id(), pos.up_id()))
        ])

    def gather_local(values):
        for c in range(3):
            pads[c] = matmul(gather_hot[c, :, :VOX], values)

    def gather_halo(field):
        at = len(halos) - 1
        for copy in halos[at]:
            copy.wait_recv()
        rows = halo_in[at]
        for c in range(3):
            pads[c] = pads[c] + matmul(gather_hot[c, :, VOX:], rows)
        field.fill([pads.at[c] for c in range(3)])

    send_hot[...] = hot(as_columns(send_rows[...].astype(jnp.float32)), VOX)
    feature_rows = twice(features[...])
    send_halo(feature_rows)

    indices[...] = jnp.full(indices.shape, float(POOL), jnp.float32)
    indices[:, :CELLS] = jnp.broadcast_to(gather_rows[...].astype(jnp.float32), (EDGE, CELLS))
    for at in range(0, 1024, LANES):
        columns[pl.ds(at, LANES), :] = as_columns(indices[0:1, at : at + LANES])
    for c in range(3):
        taken = jnp.concatenate(
            [columns[pl.ds(SPAN * row + c, EDGE), :] for row in range(SPAN * SPAN)], axis=0
        )
        gather_hot[c] = hot(taken, POOL)
    gather_local(feature_rows)
    spread_weight(first_weight, first_plain, first_flip)
    spread_weight(second_weight, second_plain, second_flip)
    for one in (first_sum, second_sum):
        for block in (BLOCKS, BLOCKS + 1):
            one.put(block, jnp.zeros((C, LANES), jnp.bfloat16))

    field_in = Field(even_in, odd_in)
    field_act = Field(even_act, odd_act)
    field_delta = Field(even_delta, odd_delta)

    gather_halo(field_in)
    first_pre = field_in.conv(first_plain)
    first_pre_ref[...] = first_pre
    first_act = (first_pre * jax.nn.sigmoid(first_pre)).astype(jnp.bfloat16)
    send_halo(first_act)
    gather_local(first_act)
    gather_halo(field_act)
    second_pre = field_act.conv(second_plain)
    sig = jax.nn.sigmoid(second_pre)
    slope = sig * (1.0 + second_pre * (1.0 - sig))
    second_delta32 = twice(cotangent[...]).astype(jnp.float32) * slope
    second_delta = second_delta32.astype(jnp.bfloat16)
    send_halo(second_delta)
    output[...] = (second_pre * sig).astype(jnp.bfloat16)[:, :C]
    weight_gradient(field_act, second_delta32, second_sum.put)
    second_sum.start_scene()
    gather_local(second_delta)
    gather_halo(field_delta)
    first_back = field_delta.conv(second_flip)
    first_pre = first_pre_ref[...]
    sig = jax.nn.sigmoid(first_pre)
    slope = sig * (1.0 + first_pre * (1.0 - sig))
    first_delta32 = first_back * slope
    first_delta = first_delta32.astype(jnp.bfloat16)
    send_halo(first_delta)
    weight_gradient(field_in, first_delta32, first_sum.put)
    first_sum.start_scene()
    second_sum.start_row()
    gather_local(first_delta)
    gather_halo(field_delta)
    second_sum.start_col()
    first_sum.start_row()
    grad_input[...] = field_delta.conv(first_flip).astype(jnp.bfloat16)[:, :C]
    second_sum.start_row_back()
    first_sum.start_col()
    second_sum.start_scene_back()
    first_sum.start_row_back()
    first_sum.start_scene_back()
    scale = float(scenes * bricks * VOX) ** (-0.5)
    second_sum.finish(grad_second, scale)
    first_sum.finish(grad_first, scale)
    for pair in halos:
        for copy in pair:
            copy.wait_send()


def shards(features, cotangent, first_weight, second_weight, send_rows, gather_rows):
    scenes, bricks = lax.axis_size("scene"), lax.axis_size("brick")
    rows, cols = brick_grid(bricks)
    field = jax.ShapeDtypeStruct((VOX, C), jnp.bfloat16)
    grad = jax.ShapeDtypeStruct((TAPS * C, C), jnp.float32)
    even = pltpu.VMEM((SPAN, SPAN * EDGE, DEEP), jnp.bfloat16)
    odd = pltpu.VMEM((SPAN, VOX // EDGE, DEEP), jnp.bfloat16)
    spread = pltpu.VMEM((PAIRS, DEEP, LANES), jnp.bfloat16)
    halo = pltpu.VMEM((EXCHANGES, LANES, LANES), jnp.bfloat16)
    scratch = [
        pltpu.VMEM((EDGE, 1024), jnp.float32),
        pltpu.VMEM((1024, LANES), jnp.float32),
        pltpu.VMEM((3, SLAB, POOL), jnp.bfloat16),
        pltpu.VMEM((LANES, VOX), jnp.bfloat16),
        pltpu.VMEM((3, SLAB, LANES), jnp.float32),
        halo,
        halo,
        pltpu.SemaphoreType.DMA((EXCHANGES, 2)),
        pltpu.SemaphoreType.DMA((EXCHANGES, 2)),
        spread, spread, spread, spread,
        even, odd, even, odd, even, odd,
        pltpu.VMEM((VOX, LANES), jnp.float32),
    ]
    out, grad_in, grad_first, grad_second = pl.pallas_call(
        functools.partial(step_kernel, scenes, bricks),
        out_shape=(field, field, grad, grad),
        in_specs=[pl.BlockSpec(memory_space=pltpu.VMEM)] * 6,
        out_specs=[pl.BlockSpec(memory_space=pltpu.VMEM)] * 4,
        scratch_shapes=scratch + Reduction.scratch(scenes, rows, cols) * 2,
        compiler_params=pltpu.CompilerParams(
            collective_id=0, has_side_effects=True, vmem_limit_bytes=48 * 1024 * 1024
        ),
    )(features[0], cotangent[0], first_weight, second_weight, send_rows, gather_rows)
    return out[None], grad_in[None], grad_first, grad_second


def solution(mesh):
    in_specs = (
        P("scene", "brick", None),
        P("scene", "brick", None),
        P(),
        P(),
        P("scene", "brick"),
        P("scene", "brick"),
    )
    out_specs = (P("scene", "brick", None), P("scene", "brick", None), P(), P())
    return jax.shard_map(shards, mesh=mesh, in_specs=in_specs, out_specs=out_specs, check_vma=False)
```

```python
import functools

import jax
import jax.numpy as jnp
from jax import lax
from jax.experimental import pallas as pl
from jax.experimental.pallas import tpu as pltpu
from jax.sharding import PartitionSpec as P

EDGE = 8
VOX = 512
C = 64
TAPS = 27
LANES = 128
MESH = pl.DeviceIdType.MESH
BLOCKS = 14
SPAN = EDGE + 2
CELLS = SPAN**3
SLAB = SPAN * SPAN * EDGE
POOL = VOX + LANES
PAIRS = 9
DEEP = 256
EXCHANGES = 4


def brick_grid(count):
    for rows in (8, 4, 2):
        if count % rows == 0 and count // rows > 1:
            return rows, count // rows
    return 1, count


class Position:
    def __init__(self, scenes, bricks):
        self.scenes = scenes
        self.bricks = bricks
        self.rows, self.cols = brick_grid(bricks)
        self.scene = lax.axis_index("scene")
        self.brick = lax.axis_index("brick")
        self.row = self.brick // self.cols
        self.col = lax.rem(self.brick, self.cols)

    def scene_peer(self, step):
        return lax.rem(self.scene + step, self.scenes)

    def row_peer(self, step):
        return lax.rem(self.row + step, self.rows)

    def col_peer(self, step):
        return lax.rem(self.col + step, self.cols)

    def scene_id(self, step):
        return (self.scene_peer(step), self.brick)

    def row_id(self, step):
        return (self.scene, self.row_peer(step) * self.cols + self.col)

    def col_id(self, step):
        return (self.scene, self.row * self.cols + self.col_peer(step))

    def down_id(self):
        return (self.scene, lax.rem(self.brick + self.bricks - 1, self.bricks))

    def up_id(self):
        return (self.scene, lax.rem(self.brick + 1, self.bricks))

    def reduce_peers(self):
        peers = [self.scene_id(k) for k in range(1, self.scenes)]
        peers += [self.row_id(k) for k in range(1, self.rows)]
        peers += [self.col_id(k) for k in range(1, self.cols)]
        return peers


def greet(peers):
    barrier = pltpu.get_barrier_semaphore()
    for peer in peers:
        pl.semaphore_signal(barrier, inc=1, device_id=peer, device_id_type=MESH)


def await_peers(peers):
    pl.semaphore_wait(pltpu.get_barrier_semaphore(), len(peers))


def remote(src, dst, send_sem, recv_sem, peer):
    copy = pltpu.make_async_remote_copy(
        src_ref=src, dst_ref=dst, send_sem=send_sem, recv_sem=recv_sem,
        device_id=peer, device_id_type=MESH,
    )
    copy.start()
    return copy


class Reduction:
    def __init__(self, pos, refs):
        self.pos = pos
        (self.send_scene, self.recv_scene, self.send_row, self.recv_row,
         self.slots, self.full, *sems) = refs
        self.sems = [(sems[2 * i], sems[2 * i + 1]) for i in range(5)]
        self.started = []

    @staticmethod
    def scratch(scenes, rows, cols):
        piece = 1024 // scenes
        small = piece // rows
        counts = (scenes, rows, cols, rows, scenes)
        sems = []
        for count in counts:
            sems += [pltpu.SemaphoreType.DMA((count - 1,))] * 2
        return [
            pltpu.VMEM((scenes, piece, LANES), jnp.bfloat16),
            pltpu.VMEM((scenes - 1, piece, LANES), jnp.bfloat16),
            pltpu.VMEM((rows, small, LANES), jnp.bfloat16),
            pltpu.VMEM((rows - 1, small, LANES), jnp.bfloat16),
            pltpu.VMEM((cols, small, LANES), jnp.bfloat16),
            pltpu.VMEM((scenes, rows, small, LANES), jnp.bfloat16),
        ] + sems

    def put(self, block, values):
        piece = self.send_scene.shape[1]
        rows = values.shape[0]
        start = block * rows
        for at in range(start, start + rows, min(rows, piece)):
            count = min(rows, piece)
            self.send_scene[at // piece, pl.ds(at % piece, count), :] = values[
                at - start : at - start + count
            ]

    def send(self, which, src, dst, peers):
        self.current = []
        for k, (peer, s, d) in enumerate(zip(peers, src, dst)):
            sems = self.sems[which]
            self.current.append(remote(s, d, sems[0].at[k], sems[1].at[k], peer))
        self.started += self.current

    def arrive(self):
        for copy in self.current:
            copy.wait_recv()

    def start_scene(self):
        pos = self.pos
        n = pos.scenes
        self.send(0, [self.send_scene.at[pos.scene_peer(k)] for k in range(1, n)],
                  [self.recv_scene.at[k - 1] for k in range(1, n)],
                  [pos.scene_id(k) for k in range(1, n)])

    def start_row(self):
        self.arrive()
        pos = self.pos
        n = pos.rows
        total = self.send_scene[pos.scene].astype(jnp.float32)
        for k in range(pos.scenes - 1):
            total = total + self.recv_scene[k].astype(jnp.float32)
        self.send_row[...] = total.astype(jnp.bfloat16).reshape(self.send_row.shape)
        self.send(1, [self.send_row.at[pos.row_peer(k)] for k in range(1, n)],
                  [self.recv_row.at[k - 1] for k in range(1, n)],
                  [pos.row_id(k) for k in range(1, n)])

    def start_col(self):
        self.arrive()
        pos = self.pos
        n = pos.cols
        total = self.send_row[pos.row].astype(jnp.float32)
        for k in range(pos.rows - 1):
            total = total + self.recv_row[k].astype(jnp.float32)
        self.slots[pos.col] = total.astype(jnp.bfloat16)
        own = self.slots.at[pos.col]
        self.send(2, [own] * (n - 1), [own] * (n - 1), [pos.col_id(k) for k in range(1, n)])

    def start_row_back(self):
        self.arrive()
        pos = self.pos
        n = pos.rows
        total = self.slots[0].astype(jnp.float32)
        for k in range(1, pos.cols):
            total = total + self.slots[k].astype(jnp.float32)
        self.full[pos.scene, pos.row] = total.astype(jnp.bfloat16)
        own = self.full.at[pos.scene, pos.row]
        self.send(3, [own] * (n - 1), [own] * (n - 1), [pos.row_id(k) for k in range(1, n)])

    def start_scene_back(self):
        self.arrive()
        pos = self.pos
        n = pos.scenes
        own = self.full.at[pos.scene]
        self.send(4, [own] * (n - 1), [own] * (n - 1), [pos.scene_id(k) for k in range(1, n)])

    def finish(self, out, scale):
        self.arrive()
        everything = self.full[...].reshape(1024, LANES)
        for block in range(BLOCKS):
            lanes = min(LANES, TAPS * C - block * LANES)
            piece = everything[block * C : (block + 1) * C].astype(jnp.float32) * scale
            out[:, block * LANES : block * LANES + lanes] = piece[:, :lanes]
        for copy in self.started:
            copy.wait_send()


def hot(columns, width):
    lane = lax.broadcasted_iota(jnp.int32, (1, LANES), 1).astype(jnp.float32)
    parts = [
        jnp.where(columns == lane + float(at), 1.0, 0.0).astype(jnp.bfloat16)
        for at in range(0, width, LANES)
    ]
    return jnp.concatenate(parts, axis=1)


def as_columns(row):
    return jnp.transpose(jnp.broadcast_to(row, (LANES, LANES)))


def twice(values):
    return jnp.concatenate([values, values], axis=1)


def matmul(left, right):
    return jnp.dot(left, right, preferred_element_type=jnp.float32)


class Field:
    def __init__(self, even, odd):
        self.even = even
        self.odd = odd

    def window(self, pair):
        a, b = pair // 3, pair % 3
        if b == 1:
            rows = self.odd[a : a + EDGE]
        else:
            rows = self.even[a : a + EDGE, EDGE * b : EDGE * b + VOX // EDGE]
        return rows.reshape(VOX, DEEP)

    def fill(self, pads):
        low = lax.broadcasted_iota(jnp.int32, (1, LANES), 1) < C
        first = jnp.where(low, pads[0][...], pads[1][...]).reshape(SPAN, SPAN * EDGE, LANES)
        last = pads[2][...].reshape(SPAN, SPAN * EDGE, LANES)
        odd = slice(EDGE, EDGE + VOX // EDGE)
        for at, part in ((0, first), (LANES, last)):
            self.even[:, :, at : at + LANES] = part.astype(jnp.bfloat16)
            self.odd[:, :, at : at + LANES] = part[:, odd].astype(jnp.bfloat16)

    def conv(self, weight):
        total = matmul(self.window(0), weight[0])
        for pair in range(1, PAIRS):
            total = total + matmul(self.window(pair), weight[pair])
        return total


def weight_gradient(field, delta, put):
    low = lax.broadcasted_iota(jnp.int32, (1, LANES), 1) < C
    turned = jnp.transpose(delta[:, :C]).astype(jnp.bfloat16)
    held = None
    for pair in range(PAIRS):
        got = matmul(turned, field.window(pair))
        first, last = got[:, :LANES], got[:, LANES:]
        block = 3 * (pair // 2)
        if pair % 2 == 0:
            put(block, first.astype(jnp.bfloat16))
            held = last
        else:
            first = jnp.concatenate([first[:, C:], first[:, :C]], axis=1)
            put(block + 1, jnp.where(low, held, first).astype(jnp.bfloat16))
            put(block + 2, jnp.where(low, first, last).astype(jnp.bfloat16))
    put(BLOCKS - 1, held.astype(jnp.bfloat16))


def upright(turned):
    return jnp.transpose(jnp.concatenate([turned, turned], axis=0))


def spread_weight(weight, plain, flip):
    zero = jnp.zeros((C, LANES), jnp.bfloat16)
    for pair in range(PAIRS):
        plain[pair, 3 * C :, :] = zero
        flip[pair, 3 * C :, :] = zero
    for at in range(0, TAPS, 2):
        taps = min(2, TAPS - at)
        stood = upright(weight[:, at * C : (at + taps) * C])
        for tap in range(at, at + taps):
            pair, c = tap // 3, tap % 3
            plain[pair, c * C : (c + 1) * C, :] = stood[(tap - at) * C : (tap - at + 1) * C]
            pair, c = (TAPS - 1 - tap) // 3, (TAPS - 1 - tap) % 3
            flip[pair, c * C : (c + 1) * C, :] = twice(weight[:, tap * C : (tap + 1) * C])


def step_kernel(
    scenes, bricks, features_in, cotangent_in, first_weight_in, second_weight_in, send_in, gather_in,
    output_out, grad_input_out, grad_first_out, grad_second_out,
    output, grad_input, grad_first, grad_second, store_sems,
    features, cotangent, first_weight, second_weight, send_rows, gather_rows, load_sems,
    indices, columns, gather_hot, send_hot, pads, halo_out, halo_in, halo_send, halo_recv,
    first_plain, first_flip, second_plain, second_flip,
    even_in, odd_in, even_act, odd_act, even_delta, odd_delta, first_pre_ref, *reduction,
):
    pos = Position(scenes, bricks)
    peers = [pos.down_id(), pos.up_id()] + pos.reduce_peers()
    loads = [
        pltpu.make_async_copy(source, target, load_sems.at[at])
        for at, (source, target) in enumerate((
            (send_in, send_rows), (features_in, features), (gather_in, gather_rows),
            (first_weight_in, first_weight), (second_weight_in, second_weight),
            (cotangent_in, cotangent),
        ))
    ]
    for load in loads:
        load.start()
    greet(peers)
    half = len(reduction) // 2
    first_sum = Reduction(pos, reduction[:half])
    second_sum = Reduction(pos, reduction[half:])
    halos = []
    stores = []

    def store(source, target):
        stores.append(pltpu.make_async_copy(source, target, store_sems.at[len(stores)]))
        stores[-1].start()

    def send_halo(values):
        at = len(halos)
        halo_out[at] = matmul(send_hot[...], values).astype(jnp.bfloat16)
        if at == 0:
            await_peers(peers)
        halos.append([
            remote(halo_out.at[at, pl.ds(64 * way, 64)], halo_in.at[at, pl.ds(64 * (1 - way), 64)],
                   halo_send.at[at, way], halo_recv.at[at, way], peer)
            for way, peer in enumerate((pos.down_id(), pos.up_id()))
        ])

    def gather_local(values):
        for c in range(3):
            pads[c] = matmul(gather_hot[c, :, :VOX], values)

    def gather_halo(field):
        at = len(halos) - 1
        for copy in halos[at]:
            copy.wait_recv()
        rows = halo_in[at]
        for c in range(3):
            pads[c] = pads[c] + matmul(gather_hot[c, :, VOX:], rows)
        field.fill([pads.at[c] for c in range(3)])

    loads[0].wait()
    send_hot[...] = hot(as_columns(send_rows[...].astype(jnp.float32)), VOX)
    loads[1].wait()
    feature_rows = upright(features[...])
    send_halo(feature_rows)
    loads[2].wait()

    indices[...] = jnp.full(indices.shape, float(POOL), jnp.float32)
    indices[:, :CELLS] = jnp.broadcast_to(gather_rows[...].astype(jnp.float32), (EDGE, CELLS))
    for at in range(0, 1024, LANES):
        columns[pl.ds(at, LANES), :] = as_columns(indices[0:1, at : at + LANES])
    for c in range(3):
        taken = jnp.concatenate(
            [columns[pl.ds(SPAN * row + c, EDGE), :] for row in range(SPAN * SPAN)], axis=0
        )
        gather_hot[c] = hot(taken, POOL)
    gather_local(feature_rows)
    loads[3].wait()
    spread_weight(first_weight, first_plain, first_flip)
    loads[4].wait()
    spread_weight(second_weight, second_plain, second_flip)
    for one in (first_sum, second_sum):
        for block in (BLOCKS, BLOCKS + 1):
            one.put(block, jnp.zeros((C, LANES), jnp.bfloat16))

    loads[5].wait()
    cot = upright(cotangent[...]).astype(jnp.float32)
    field_in = Field(even_in, odd_in)
    field_act = Field(even_act, odd_act)
    field_delta = Field(even_delta, odd_delta)

    gather_halo(field_in)
    first_pre = field_in.conv(first_plain)
    first_pre_ref[...] = first_pre
    first_act = (first_pre * jax.nn.sigmoid(first_pre)).astype(jnp.bfloat16)
    send_halo(first_act)
    gather_local(first_act)
    gather_halo(field_act)
    second_pre = field_act.conv(second_plain)
    sig = jax.nn.sigmoid(second_pre)
    slope = sig * (1.0 + second_pre * (1.0 - sig))
    second_delta32 = cot * slope
    second_delta = second_delta32.astype(jnp.bfloat16)
    send_halo(second_delta)
    output[...] = jnp.transpose(second_pre * sig)[:C].astype(jnp.bfloat16)
    store(output, output_out)
    weight_gradient(field_act, second_delta32, second_sum.put)
    second_sum.start_scene()
    gather_local(second_delta)
    gather_halo(field_delta)
    first_back = field_delta.conv(second_flip)
    first_pre = first_pre_ref[...]
    sig = jax.nn.sigmoid(first_pre)
    slope = sig * (1.0 + first_pre * (1.0 - sig))
    first_delta32 = first_back * slope
    first_delta = first_delta32.astype(jnp.bfloat16)
    send_halo(first_delta)
    weight_gradient(field_in, first_delta32, first_sum.put)
    first_sum.start_scene()
    second_sum.start_row()
    gather_local(first_delta)
    gather_halo(field_delta)
    second_sum.start_col()
    first_sum.start_row()
    grad_input[...] = jnp.transpose(field_delta.conv(first_flip))[:C].astype(jnp.bfloat16)
    store(grad_input, grad_input_out)
    second_sum.start_row_back()
    first_sum.start_col()
    second_sum.start_scene_back()
    first_sum.start_row_back()
    first_sum.start_scene_back()
    scale = float(scenes * bricks * VOX) ** (-0.5)
    second_sum.finish(grad_second, scale)
    store(grad_second, grad_second_out)
    first_sum.finish(grad_first, scale)
    store(grad_first, grad_first_out)
    for copy in stores:
        copy.wait()
    for pair in halos:
        for copy in pair:
            copy.wait_send()


def hand_over(*refs):
    count = 4
    sources, targets, held = refs[:count], refs[count : 2 * count], refs[2 * count : 3 * count]
    load_sems, store_sems = refs[3 * count :]
    loads = [pltpu.make_async_copy(sources[at], held[at], load_sems.at[at]) for at in range(count)]
    stores = [pltpu.make_async_copy(held[at], targets[at], store_sems.at[at]) for at in range(count)]
    for load in loads:
        load.start()
    for load, store in zip(loads, stores):
        load.wait()
        store.start()
    for store in stores:
        store.wait()


def shards(features, cotangent, first_weight, second_weight, send_rows, gather_rows):
    scenes, bricks = lax.axis_size("scene"), lax.axis_size("brick")
    rows, cols = brick_grid(bricks)
    field = jax.ShapeDtypeStruct((C, VOX), jnp.bfloat16)
    grad = jax.ShapeDtypeStruct((C, TAPS * C), jnp.float32)
    operands = [features[0].T, cotangent[0].T, first_weight.T, second_weight.T, send_rows, gather_rows]
    even = pltpu.VMEM((SPAN, SPAN * EDGE, DEEP), jnp.bfloat16)
    odd = pltpu.VMEM((SPAN, VOX // EDGE, DEEP), jnp.bfloat16)
    spread = pltpu.VMEM((PAIRS, DEEP, LANES), jnp.bfloat16)
    halo = pltpu.VMEM((EXCHANGES, LANES, LANES), jnp.bfloat16)
    results = [pltpu.VMEM(one.shape, one.dtype) for one in (field, field, grad, grad)]
    results.append(pltpu.SemaphoreType.DMA((4,)))
    scratch = results + [pltpu.VMEM(one.shape, one.dtype) for one in operands] + [
        pltpu.SemaphoreType.DMA((len(operands),)),
        pltpu.VMEM((EDGE, 1024), jnp.float32),
        pltpu.VMEM((1024, LANES), jnp.float32),
        pltpu.VMEM((3, SLAB, POOL), jnp.bfloat16),
        pltpu.VMEM((LANES, VOX), jnp.bfloat16),
        pltpu.VMEM((3, SLAB, LANES), jnp.float32),
        halo,
        halo,
        pltpu.SemaphoreType.DMA((EXCHANGES, 2)),
        pltpu.SemaphoreType.DMA((EXCHANGES, 2)),
        spread, spread, spread, spread,
        even, odd, even, odd, even, odd,
        pltpu.VMEM((VOX, LANES), jnp.float32),
    ]
    out, grad_in, grad_first, grad_second = pl.pallas_call(
        functools.partial(step_kernel, scenes, bricks),
        out_shape=(field, field, grad, grad),
        in_specs=[pl.BlockSpec(memory_space=pltpu.HBM)] * 6,
        out_specs=[pl.BlockSpec(memory_space=pltpu.HBM)] * 4,
        scratch_shapes=scratch + Reduction.scratch(scenes, rows, cols) * 2,
        compiler_params=pltpu.CompilerParams(
            collective_id=0, has_side_effects=True, vmem_limit_bytes=62 * 1024 * 1024
        ),
    )(*operands)
    out, grad_in, grad_first, grad_second = pl.pallas_call(
        hand_over,
        out_shape=(field, field, grad, grad),
        in_specs=[pl.BlockSpec(memory_space=pltpu.HBM)] * 4,
        out_specs=[pl.BlockSpec(memory_space=pltpu.HBM)] * 4,
        scratch_shapes=results[:4] + [pltpu.SemaphoreType.DMA((4,))] * 2,
        compiler_params=pltpu.CompilerParams(vmem_limit_bytes=62 * 1024 * 1024),
    )(out, grad_in, grad_first, grad_second)
    return out.T[None], grad_in.T[None], grad_first.T, grad_second.T


def solution(mesh):
    in_specs = (
        P("scene", "brick", None),
        P("scene", "brick", None),
        P(),
        P(),
        P("scene", "brick"),
        P("scene", "brick"),
    )
    out_specs = (P("scene", "brick", None), P("scene", "brick", None), P(), P())
    return jax.shard_map(shards, mesh=mesh, in_specs=in_specs, out_specs=out_specs, check_vma=False)
```

```python
import functools

import jax
import jax.numpy as jnp
from jax import lax
from jax.experimental import pallas as pl
from jax.experimental.pallas import tpu as pltpu
from jax.sharding import PartitionSpec as P

EDGE = 8
VOX = 512
C = 64
TAPS = 27
LANES = 128
MESH = pl.DeviceIdType.MESH
BLOCKS = 14
SPAN = EDGE + 2
CELLS = SPAN**3
SLAB = SPAN * SPAN * EDGE
POOL = VOX + LANES
PAIRS = 9
DEEP = 256
EXCHANGES = 4


def brick_grid(count):
    for rows in (8, 4, 2):
        if count % rows == 0 and count // rows > 1:
            return rows, count // rows
    return 1, count


def far_first(count):
    return sorted(range(1, count), key=lambda step: (-min(step, count - step), step))


class Position:
    def __init__(self, scenes, bricks):
        self.scenes = scenes
        self.bricks = bricks
        self.rows, self.cols = brick_grid(bricks)
        self.scene = lax.axis_index("scene")
        self.brick = lax.axis_index("brick")
        self.row = self.brick // self.cols
        self.col = lax.rem(self.brick, self.cols)

    def scene_peer(self, step):
        return lax.rem(self.scene + step, self.scenes)

    def row_peer(self, step):
        return lax.rem(self.row + step, self.rows)

    def col_peer(self, step):
        return lax.rem(self.col + step, self.cols)

    def scene_id(self, step):
        return (self.scene_peer(step), self.brick)

    def row_id(self, step):
        return (self.scene, self.row_peer(step) * self.cols + self.col)

    def col_id(self, step):
        return (self.scene, self.row * self.cols + self.col_peer(step))

    def down_id(self):
        return (self.scene, lax.rem(self.brick + self.bricks - 1, self.bricks))

    def up_id(self):
        return (self.scene, lax.rem(self.brick + 1, self.bricks))

    def reduce_peers(self):
        peers = [self.scene_id(k) for k in range(1, self.scenes)]
        peers += [self.row_id(k) for k in range(1, self.rows)]
        peers += [self.col_id(k) for k in range(1, self.cols)]
        return peers


def greet(peers):
    barrier = pltpu.get_barrier_semaphore()
    for peer in peers:
        pl.semaphore_signal(barrier, inc=1, device_id=peer, device_id_type=MESH)


def await_peers(peers):
    pl.semaphore_wait(pltpu.get_barrier_semaphore(), len(peers))


def remote(src, dst, send_sem, recv_sem, peer):
    copy = pltpu.make_async_remote_copy(
        src_ref=src, dst_ref=dst, send_sem=send_sem, recv_sem=recv_sem,
        device_id=peer, device_id_type=MESH,
    )
    copy.start()
    return copy


class Reduction:
    def __init__(self, pos, refs):
        self.pos = pos
        (self.send_scene, self.recv_scene, self.send_row, self.recv_row,
         self.slots, self.full, *sems) = refs
        self.sems = [(sems[2 * i], sems[2 * i + 1]) for i in range(5)]
        self.started = []

    @staticmethod
    def scratch(scenes, rows, cols):
        piece = 1024 // scenes
        small = piece // rows
        counts = (scenes, rows, cols, rows, scenes)
        sems = []
        for count in counts:
            sems += [pltpu.SemaphoreType.DMA((count - 1,))] * 2
        return [
            pltpu.VMEM((scenes, piece, LANES), jnp.bfloat16),
            pltpu.VMEM((scenes - 1, piece, LANES), jnp.bfloat16),
            pltpu.VMEM((rows, small, LANES), jnp.bfloat16),
            pltpu.VMEM((rows - 1, small, LANES), jnp.bfloat16),
            pltpu.VMEM((cols, small, LANES), jnp.bfloat16),
            pltpu.VMEM((scenes, rows, small, LANES), jnp.bfloat16),
        ] + sems

    def put(self, block, values):
        piece = self.send_scene.shape[1]
        rows = values.shape[0]
        start = block * rows
        for at in range(start, start + rows, min(rows, piece)):
            count = min(rows, piece)
            self.send_scene[at // piece, pl.ds(at % piece, count), :] = values[
                at - start : at - start + count
            ]

    def send(self, which, src, dst, peers):
        sems = self.sems[which]
        self.current = [
            remote(src[step - 1], dst[step - 1], sems[0].at[step - 1], sems[1].at[step - 1],
                   peers[step - 1])
            for step in far_first(len(peers) + 1)
        ]
        self.started += self.current

    def arrive(self):
        for copy in self.current:
            copy.wait_recv()

    def start_scene(self):
        pos = self.pos
        n = pos.scenes
        self.send(0, [self.send_scene.at[pos.scene_peer(k)] for k in range(1, n)],
                  [self.recv_scene.at[k - 1] for k in range(1, n)],
                  [pos.scene_id(k) for k in range(1, n)])

    def start_row(self):
        self.arrive()
        pos = self.pos
        n = pos.rows
        total = self.send_scene[pos.scene].astype(jnp.float32)
        for k in range(pos.scenes - 1):
            total = total + self.recv_scene[k].astype(jnp.float32)
        self.send_row[...] = total.astype(jnp.bfloat16).reshape(self.send_row.shape)
        self.send(1, [self.send_row.at[pos.row_peer(k)] for k in range(1, n)],
                  [self.recv_row.at[k - 1] for k in range(1, n)],
                  [pos.row_id(k) for k in range(1, n)])

    def start_col(self):
        self.arrive()
        pos = self.pos
        n = pos.cols
        total = self.send_row[pos.row].astype(jnp.float32)
        for k in range(pos.rows - 1):
            total = total + self.recv_row[k].astype(jnp.float32)
        self.slots[pos.col] = total.astype(jnp.bfloat16)
        own = self.slots.at[pos.col]
        self.send(2, [own] * (n - 1), [own] * (n - 1), [pos.col_id(k) for k in range(1, n)])

    def start_row_back(self):
        self.arrive()
        pos = self.pos
        n = pos.rows
        total = self.slots[0].astype(jnp.float32)
        for k in range(1, pos.cols):
            total = total + self.slots[k].astype(jnp.float32)
        self.full[pos.scene, pos.row] = total.astype(jnp.bfloat16)
        own = self.full.at[pos.scene, pos.row]
        self.send(3, [own] * (n - 1), [own] * (n - 1), [pos.row_id(k) for k in range(1, n)])

    def start_scene_back(self):
        self.arrive()
        pos = self.pos
        n = pos.scenes
        own = self.full.at[pos.scene]
        self.send(4, [own] * (n - 1), [own] * (n - 1), [pos.scene_id(k) for k in range(1, n)])

    def finish(self, out, scale):
        self.arrive()
        everything = self.full[...].reshape(1024, LANES)
        for block in range(BLOCKS):
            lanes = min(LANES, TAPS * C - block * LANES)
            piece = everything[block * C : (block + 1) * C].astype(jnp.float32) * scale
            out[:, block * LANES : block * LANES + lanes] = piece[:, :lanes]
        for copy in self.started:
            copy.wait_send()


def hot(columns, width):
    lane = lax.broadcasted_iota(jnp.int32, (1, LANES), 1).astype(jnp.float32)
    parts = [
        jnp.where(columns == lane + float(at), 1.0, 0.0).astype(jnp.bfloat16)
        for at in range(0, width, LANES)
    ]
    return jnp.concatenate(parts, axis=1)


def as_columns(row):
    return jnp.transpose(jnp.broadcast_to(row, (LANES, LANES)))


def twice(values):
    return jnp.concatenate([values, values], axis=1)


def matmul(left, right):
    return jnp.dot(left, right, preferred_element_type=jnp.float32)


class Field:
    def __init__(self, even, odd):
        self.even = even
        self.odd = odd

    def window(self, pair):
        a, b = pair // 3, pair % 3
        if b == 1:
            rows = self.odd[a : a + EDGE]
        else:
            rows = self.even[a : a + EDGE, EDGE * b : EDGE * b + VOX // EDGE]
        return rows.reshape(VOX, DEEP)

    def fill(self, pads, halo_hot, rows):
        low = lax.broadcasted_iota(jnp.int32, (1, LANES), 1) < C
        for plane in range(0, SPAN, 2):
            span = slice(plane * SPAN * EDGE, (plane + 2) * SPAN * EDGE)
            cells = [pads[c, span] + matmul(halo_hot[c, span, VOX:], rows) for c in range(3)]
            for lane, values in ((0, jnp.where(low, cells[0], cells[1])), (LANES, cells[2])):
                for half in range(2):
                    part = values[half * SPAN * EDGE : (half + 1) * SPAN * EDGE]
                    self.even[plane + half, :, lane : lane + LANES] = part.astype(jnp.bfloat16)
                    self.odd[plane + half, :, lane : lane + LANES] = part[
                        EDGE : EDGE + VOX // EDGE
                    ].astype(jnp.bfloat16)

    def conv(self, weight):
        rows = VOX // 2
        parts = []
        for at in range(2):
            total = matmul(self.window(0)[at * rows : (at + 1) * rows], weight[0])
            for pair in range(1, PAIRS):
                total = total + matmul(self.window(pair)[at * rows : (at + 1) * rows], weight[pair])
            parts.append(total)
        return jnp.concatenate(parts, axis=0)


def weight_gradient(field, delta, put):
    low = lax.broadcasted_iota(jnp.int32, (1, LANES), 1) < C
    turned = jnp.transpose(delta[:, :C]).astype(jnp.bfloat16)
    held = None
    for pair in range(PAIRS):
        got = matmul(turned, field.window(pair))
        first, last = got[:, :LANES], got[:, LANES:]
        block = 3 * (pair // 2)
        if pair % 2 == 0:
            put(block, first.astype(jnp.bfloat16))
            held = last
        else:
            first = jnp.concatenate([first[:, C:], first[:, :C]], axis=1)
            put(block + 1, jnp.where(low, held, first).astype(jnp.bfloat16))
            put(block + 2, jnp.where(low, first, last).astype(jnp.bfloat16))
    put(BLOCKS - 1, held.astype(jnp.bfloat16))


def upright(turned):
    return jnp.transpose(jnp.concatenate([turned, turned], axis=0))


def spread_plain(weight, plain):
    for pair in range(PAIRS):
        plain[pair, 3 * C :, :] = jnp.zeros((C, LANES), jnp.bfloat16)
    for at in range(0, TAPS, 2):
        taps = min(2, TAPS - at)
        stood = upright(weight[:, at * C : (at + taps) * C])
        for tap in range(at, at + taps):
            pair, c = tap // 3, tap % 3
            plain[pair, c * C : (c + 1) * C, :] = stood[(tap - at) * C : (tap - at + 1) * C]


def spread_flip(weight, flip):
    for pair in range(PAIRS):
        flip[pair, 3 * C :, :] = jnp.zeros((C, LANES), jnp.bfloat16)
    for tap in range(TAPS):
        pair, c = (TAPS - 1 - tap) // 3, (TAPS - 1 - tap) % 3
        flip[pair, c * C : (c + 1) * C, :] = twice(weight[:, tap * C : (tap + 1) * C])


def step_kernel(
    scenes, bricks, features_in, cotangent_in, first_weight_in, second_weight_in, send_in, gather_in,
    output_out, grad_input_out, grad_first_out, grad_second_out,
    output, grad_input, grad_first, grad_second, store_sems,
    features, cotangent, first_weight, second_weight, send_rows, gather_rows, load_sems,
    indices, columns, gather_hot, send_hot, pads, halo_out, halo_in, halo_send, halo_recv,
    first_plain, first_flip, second_plain, second_flip,
    even_in, odd_in, even_act, odd_act, even_delta, odd_delta, first_slope, *reduction,
):
    pos = Position(scenes, bricks)
    peers = [pos.down_id(), pos.up_id()] + pos.reduce_peers()
    loads = [
        pltpu.make_async_copy(source, target, load_sems.at[at])
        for at, (source, target) in enumerate((
            (send_in, send_rows), (features_in, features), (gather_in, gather_rows),
            (first_weight_in, first_weight), (second_weight_in, second_weight),
            (cotangent_in, cotangent),
        ))
    ]
    for load in loads:
        load.start()
    greet(peers)
    half = len(reduction) // 2
    first_sum = Reduction(pos, reduction[:half])
    second_sum = Reduction(pos, reduction[half:])
    halos = []
    stores = []

    def store(source, target):
        stores.append(pltpu.make_async_copy(source, target, store_sems.at[len(stores)]))
        stores[-1].start()

    def send_halo(values):
        at = len(halos)
        halo_out[at] = matmul(send_hot[...], values).astype(jnp.bfloat16)
        if at == 0:
            await_peers(peers)
        halos.append([
            remote(halo_out.at[at, pl.ds(64 * way, 64)], halo_in.at[at, pl.ds(64 * (1 - way), 64)],
                   halo_send.at[at, way], halo_recv.at[at, way], peer)
            for way, peer in enumerate((pos.down_id(), pos.up_id()))
        ])

    def gather_local(values):
        for c in range(3):
            for at in range(0, SLAB, 160):
                pads[c, at : at + 160] = matmul(gather_hot[c, at : at + 160, :VOX], values)

    def gather_halo(field):
        at = len(halos) - 1
        for copy in halos[at]:
            copy.wait_recv()
        rows = halo_in[at]
        field.fill(pads, gather_hot, rows)

    loads[0].wait()
    send_hot[...] = hot(as_columns(send_rows[...].astype(jnp.float32)), VOX)
    loads[1].wait()
    feature_rows = upright(features[...])
    loads[2].wait()

    indices[...] = jnp.full(indices.shape, float(POOL), jnp.float32)
    indices[:, :CELLS] = jnp.broadcast_to(gather_rows[...].astype(jnp.float32), (EDGE, CELLS))
    for at in range(0, 1024, LANES):
        columns[pl.ds(at, LANES), :] = as_columns(indices[0:1, at : at + LANES])
    for c in range(3):
        taken = jnp.concatenate(
            [columns[pl.ds(SPAN * row + c, EDGE), :] for row in range(SPAN * SPAN)], axis=0
        )
        gather_hot[c] = hot(taken, POOL)
    send_halo(feature_rows)
    gather_local(feature_rows)
    loads[3].wait()
    spread_plain(first_weight, first_plain)
    for one in (first_sum, second_sum):
        for block in (BLOCKS, BLOCKS + 1):
            one.put(block, jnp.zeros((C, LANES), jnp.bfloat16))

    field_in = Field(even_in, odd_in)
    field_act = Field(even_act, odd_act)
    field_delta = Field(even_delta, odd_delta)

    gather_halo(field_in)
    first_pre = field_in.conv(first_plain)
    sig = jax.nn.sigmoid(first_pre)
    first_act = (first_pre * sig).astype(jnp.bfloat16)
    send_halo(first_act)
    gather_local(first_act)
    first_slope[...] = sig * (1.0 + first_pre * (1.0 - sig))
    loads[4].wait()
    spread_plain(second_weight, second_plain)
    loads[5].wait()
    cot = upright(cotangent[...]).astype(jnp.float32)
    gather_halo(field_act)
    second_pre = field_act.conv(second_plain)
    sig = jax.nn.sigmoid(second_pre)
    slope = sig * (1.0 + second_pre * (1.0 - sig))
    second_delta32 = cot * slope
    second_delta = second_delta32.astype(jnp.bfloat16)
    send_halo(second_delta)
    weight_gradient(field_act, second_delta32, second_sum.put)
    second_sum.start_scene()
    gather_local(second_delta)
    spread_flip(second_weight, second_flip)
    output[...] = jnp.transpose(second_pre * sig)[:C].astype(jnp.bfloat16)
    store(output, output_out)
    gather_halo(field_delta)
    first_delta32 = field_delta.conv(second_flip) * first_slope[...]
    weight_gradient(field_in, first_delta32, first_sum.put)
    first_sum.start_scene()
    first_delta = first_delta32.astype(jnp.bfloat16)
    send_halo(first_delta)
    spread_flip(first_weight, first_flip)
    gather_local(first_delta)
    second_sum.start_row()
    gather_halo(field_delta)
    second_sum.start_col()
    first_sum.start_row()
    grad_input[...] = jnp.transpose(field_delta.conv(first_flip))[:C].astype(jnp.bfloat16)
    store(grad_input, grad_input_out)
    first_sum.start_col()
    second_sum.start_row_back()
    second_sum.start_scene_back()
    first_sum.start_row_back()
    first_sum.start_scene_back()
    scale = float(scenes * bricks * VOX) ** (-0.5)
    second_sum.finish(grad_second, scale)
    store(grad_second, grad_second_out)
    first_sum.finish(grad_first, scale)
    store(grad_first, grad_first_out)
    for copy in stores:
        copy.wait()
    for pair in halos:
        for copy in pair:
            copy.wait_send()


def hand_over(*refs):
    count = 4
    sources, targets, held = refs[:count], refs[count : 2 * count], refs[2 * count : 3 * count]
    load_sems, store_sems = refs[3 * count :]
    loads = [pltpu.make_async_copy(sources[at], held[at], load_sems.at[at]) for at in range(count)]
    stores = [pltpu.make_async_copy(held[at], targets[at], store_sems.at[at]) for at in range(count)]
    for load in loads:
        load.start()
    for load, store in zip(loads, stores):
        load.wait()
        store.start()
    for store in stores:
        store.wait()


def shards(features, cotangent, first_weight, second_weight, send_rows, gather_rows):
    scenes, bricks = lax.axis_size("scene"), lax.axis_size("brick")
    rows, cols = brick_grid(bricks)
    field = jax.ShapeDtypeStruct((C, VOX), jnp.bfloat16)
    grad = jax.ShapeDtypeStruct((C, TAPS * C), jnp.float32)
    operands = [features[0].T, cotangent[0].T, first_weight.T, second_weight.T, send_rows, gather_rows]
    even = pltpu.VMEM((SPAN, SPAN * EDGE, DEEP), jnp.bfloat16)
    odd = pltpu.VMEM((SPAN, VOX // EDGE, DEEP), jnp.bfloat16)
    spread = pltpu.VMEM((PAIRS, DEEP, LANES), jnp.bfloat16)
    halo = pltpu.VMEM((EXCHANGES, LANES, LANES), jnp.bfloat16)
    results = [pltpu.VMEM(one.shape, one.dtype) for one in (field, field, grad, grad)]
    results.append(pltpu.SemaphoreType.DMA((4,)))
    scratch = results + [pltpu.VMEM(one.shape, one.dtype) for one in operands] + [
        pltpu.SemaphoreType.DMA((len(operands),)),
        pltpu.VMEM((EDGE, 1024), jnp.float32),
        pltpu.VMEM((1024, LANES), jnp.float32),
        pltpu.VMEM((3, SLAB, POOL), jnp.bfloat16),
        pltpu.VMEM((LANES, VOX), jnp.bfloat16),
        pltpu.VMEM((3, SLAB, LANES), jnp.float32),
        halo,
        halo,
        pltpu.SemaphoreType.DMA((EXCHANGES, 2)),
        pltpu.SemaphoreType.DMA((EXCHANGES, 2)),
        spread, spread, spread, spread,
        even, odd, even, odd, even, odd,
        pltpu.VMEM((VOX, LANES), jnp.float32),
    ]
    out, grad_in, grad_first, grad_second = pl.pallas_call(
        functools.partial(step_kernel, scenes, bricks),
        out_shape=(field, field, grad, grad),
        in_specs=[pl.BlockSpec(memory_space=pltpu.HBM)] * 6,
        out_specs=[pl.BlockSpec(memory_space=pltpu.HBM)] * 4,
        scratch_shapes=scratch + Reduction.scratch(scenes, rows, cols) * 2,
        compiler_params=pltpu.CompilerParams(
            collective_id=0, has_side_effects=True, vmem_limit_bytes=62 * 1024 * 1024
        ),
    )(*operands)
    out, grad_in, grad_first, grad_second = pl.pallas_call(
        hand_over,
        out_shape=(field, field, grad, grad),
        in_specs=[pl.BlockSpec(memory_space=pltpu.HBM)] * 4,
        out_specs=[pl.BlockSpec(memory_space=pltpu.HBM)] * 4,
        scratch_shapes=results[:4] + [pltpu.SemaphoreType.DMA((4,))] * 2,
        compiler_params=pltpu.CompilerParams(vmem_limit_bytes=62 * 1024 * 1024),
    )(out, grad_in, grad_first, grad_second)
    return out.T[None], grad_in.T[None], grad_first.T, grad_second.T


def solution(mesh):
    in_specs = (
        P("scene", "brick", None),
        P("scene", "brick", None),
        P(),
        P(),
        P("scene", "brick"),
        P("scene", "brick"),
    )
    out_specs = (P("scene", "brick", None), P("scene", "brick", None), P(), P())
    return jax.shard_map(shards, mesh=mesh, in_specs=in_specs, out_specs=out_specs, check_vma=False)
```

```python
import functools

import jax
import jax.numpy as jnp
from jax import lax
from jax.experimental import pallas as pl
from jax.experimental.pallas import tpu as pltpu
from jax.sharding import PartitionSpec as P

EDGE = 8
VOX = 512
C = 64
TAPS = 27
LANES = 128
MESH = pl.DeviceIdType.MESH
BLOCKS = 14
SPAN = EDGE + 2
CELLS = SPAN**3
SLAB = SPAN * SPAN * EDGE
POOL = VOX + LANES
PAIRS = 9
DEEP = 256
EXCHANGES = 4


def brick_grid(count):
    for rows in (8, 4, 2):
        if count % rows == 0 and count // rows > 1:
            return rows, count // rows
    return 1, count


def far_first(count):
    return sorted(range(1, count), key=lambda step: (-min(step, count - step), step))


class Position:
    def __init__(self, scenes, bricks):
        self.scenes = scenes
        self.bricks = bricks
        self.rows, self.cols = brick_grid(bricks)
        self.scene = lax.axis_index("scene")
        self.brick = lax.axis_index("brick")
        self.row = self.brick // self.cols
        self.col = lax.rem(self.brick, self.cols)

    def scene_peer(self, step):
        return lax.rem(self.scene + step, self.scenes)

    def row_peer(self, step):
        return lax.rem(self.row + step, self.rows)

    def col_peer(self, step):
        return lax.rem(self.col + step, self.cols)

    def scene_id(self, step):
        return (self.scene_peer(step), self.brick)

    def row_id(self, step):
        return (self.scene, self.row_peer(step) * self.cols + self.col)

    def col_id(self, step):
        return (self.scene, self.row * self.cols + self.col_peer(step))

    def down_id(self):
        return (self.scene, lax.rem(self.brick + self.bricks - 1, self.bricks))

    def up_id(self):
        return (self.scene, lax.rem(self.brick + 1, self.bricks))

    def near_peers(self):
        peers = [self.down_id(), self.up_id()] + self.row_pair(1) + self.col_pair(1)
        return peers + [self.scene_id(k) for k in far_first(self.scenes)]

    def row_pair(self, step):
        return [self.row_id(step), self.row_id(self.rows - step)]

    def col_pair(self, step):
        return [self.col_id(step), self.col_id(self.cols - step)]


class Word:
    def __init__(self, pos, sems):
        self.rounds = [
            [(sems.at[0], pos.col_pair(1)), (sems.at[1], pos.row_pair(1))],
            [(sems.at[2], pos.col_pair(2)), (sems.at[3], pos.row_pair(2))],
            [(sems.at[4], pos.col_pair(4))],
        ]

    def give(self, at):
        for sem, peers in self.rounds[at]:
            for peer in peers:
                pl.semaphore_signal(sem, inc=1, device_id=peer, device_id_type=MESH)

    def take(self, at):
        for sem, peers in self.rounds[at]:
            pl.semaphore_wait(sem, len(peers))


def greet(peers):
    barrier = pltpu.get_barrier_semaphore()
    for peer in peers:
        pl.semaphore_signal(barrier, inc=1, device_id=peer, device_id_type=MESH)


def await_peers(peers):
    pl.semaphore_wait(pltpu.get_barrier_semaphore(), len(peers))


def remote(src, dst, send_sem, recv_sem, peer):
    copy = pltpu.make_async_remote_copy(
        src_ref=src, dst_ref=dst, send_sem=send_sem, recv_sem=recv_sem,
        device_id=peer, device_id_type=MESH,
    )
    copy.start()
    return copy


class Reduction:
    def __init__(self, pos, refs):
        self.pos = pos
        (self.send_scene, self.recv_scene, self.send_row, self.recv_row,
         self.slots, self.full, *sems) = refs
        self.sems = [(sems[2 * i], sems[2 * i + 1]) for i in range(5)]
        self.started = []

    @staticmethod
    def scratch(scenes, rows, cols):
        piece = 1024 // scenes
        small = piece // rows
        counts = (scenes, rows, cols, rows, scenes)
        sems = []
        for count in counts:
            sems += [pltpu.SemaphoreType.DMA((count - 1,))] * 2
        return [
            pltpu.VMEM((scenes, piece, LANES), jnp.bfloat16),
            pltpu.VMEM((scenes - 1, piece, LANES), jnp.bfloat16),
            pltpu.VMEM((rows, small, LANES), jnp.bfloat16),
            pltpu.VMEM((rows - 1, small, LANES), jnp.bfloat16),
            pltpu.VMEM((cols, small, LANES), jnp.bfloat16),
            pltpu.VMEM((scenes, rows, small, LANES), jnp.bfloat16),
        ] + sems

    def put(self, block, values):
        piece = self.send_scene.shape[1]
        rows = values.shape[0]
        start = block * rows
        for at in range(start, start + rows, min(rows, piece)):
            count = min(rows, piece)
            self.send_scene[at // piece, pl.ds(at % piece, count), :] = values[
                at - start : at - start + count
            ]

    def send(self, which, src, dst, peers):
        sems = self.sems[which]
        self.current = [
            remote(src[step - 1], dst[step - 1], sems[0].at[step - 1], sems[1].at[step - 1],
                   peers[step - 1])
            for step in far_first(len(peers) + 1)
        ]
        self.started += self.current

    def arrive(self):
        for copy in self.current:
            copy.wait_recv()

    def start_scene(self):
        pos = self.pos
        n = pos.scenes
        self.send(0, [self.send_scene.at[pos.scene_peer(k)] for k in range(1, n)],
                  [self.recv_scene.at[k - 1] for k in range(1, n)],
                  [pos.scene_id(k) for k in range(1, n)])

    def start_row(self):
        self.arrive()
        pos = self.pos
        n = pos.rows
        total = self.send_scene[pos.scene].astype(jnp.float32)
        for k in range(pos.scenes - 1):
            total = total + self.recv_scene[k].astype(jnp.float32)
        self.send_row[...] = total.astype(jnp.bfloat16).reshape(self.send_row.shape)
        self.send(1, [self.send_row.at[pos.row_peer(k)] for k in range(1, n)],
                  [self.recv_row.at[k - 1] for k in range(1, n)],
                  [pos.row_id(k) for k in range(1, n)])

    def start_col(self):
        self.arrive()
        pos = self.pos
        n = pos.cols
        total = self.send_row[pos.row].astype(jnp.float32)
        for k in range(pos.rows - 1):
            total = total + self.recv_row[k].astype(jnp.float32)
        self.slots[pos.col] = total.astype(jnp.bfloat16)
        own = self.slots.at[pos.col]
        self.send(2, [own] * (n - 1), [own] * (n - 1), [pos.col_id(k) for k in range(1, n)])

    def start_row_back(self):
        self.arrive()
        pos = self.pos
        n = pos.rows
        total = self.slots[0].astype(jnp.float32)
        for k in range(1, pos.cols):
            total = total + self.slots[k].astype(jnp.float32)
        self.full[pos.scene, pos.row] = total.astype(jnp.bfloat16)
        own = self.full.at[pos.scene, pos.row]
        self.send(3, [own] * (n - 1), [own] * (n - 1), [pos.row_id(k) for k in range(1, n)])

    def start_scene_back(self):
        self.arrive()
        pos = self.pos
        n = pos.scenes
        own = self.full.at[pos.scene]
        self.send(4, [own] * (n - 1), [own] * (n - 1), [pos.scene_id(k) for k in range(1, n)])

    def finish(self, out, scale):
        self.arrive()
        everything = self.full[...].reshape(1024, LANES)
        for block in range(BLOCKS):
            lanes = min(LANES, TAPS * C - block * LANES)
            piece = everything[block * C : (block + 1) * C].astype(jnp.float32) * scale
            out[:, block * LANES : block * LANES + lanes] = piece[:, :lanes]
        for copy in self.started:
            copy.wait_send()


def hot(columns, width):
    lane = lax.broadcasted_iota(jnp.int32, (1, LANES), 1).astype(jnp.float32)
    parts = [
        jnp.where(columns == lane + float(at), 1.0, 0.0).astype(jnp.bfloat16)
        for at in range(0, width, LANES)
    ]
    return jnp.concatenate(parts, axis=1)


def as_columns(row):
    return jnp.transpose(jnp.broadcast_to(row, (LANES, LANES)))


def twice(values):
    return jnp.concatenate([values, values], axis=1)


def matmul(left, right):
    return jnp.dot(left, right, preferred_element_type=jnp.float32)


class Field:
    def __init__(self, even, odd):
        self.even = even
        self.odd = odd

    def window(self, pair):
        a, b = pair // 3, pair % 3
        if b == 1:
            rows = self.odd[a : a + EDGE]
        else:
            rows = self.even[a : a + EDGE, EDGE * b : EDGE * b + VOX // EDGE]
        return rows.reshape(VOX, DEEP)

    def fill(self, pads, halo_hot, rows):
        low = lax.broadcasted_iota(jnp.int32, (1, LANES), 1) < C
        for plane in range(0, SPAN, 2):
            span = slice(plane * SPAN * EDGE, (plane + 2) * SPAN * EDGE)
            cells = [pads[c, span] + matmul(halo_hot[c, span, VOX:], rows) for c in range(3)]
            for lane, values in ((0, jnp.where(low, cells[0], cells[1])), (LANES, cells[2])):
                for half in range(2):
                    part = values[half * SPAN * EDGE : (half + 1) * SPAN * EDGE]
                    self.even[plane + half, :, lane : lane + LANES] = part.astype(jnp.bfloat16)
                    self.odd[plane + half, :, lane : lane + LANES] = part[
                        EDGE : EDGE + VOX // EDGE
                    ].astype(jnp.bfloat16)

    def conv(self, weight):
        rows = VOX // 2
        parts = []
        for at in range(2):
            total = matmul(self.window(0)[at * rows : (at + 1) * rows], weight[0])
            for pair in range(1, PAIRS):
                total = total + matmul(self.window(pair)[at * rows : (at + 1) * rows], weight[pair])
            parts.append(total)
        return jnp.concatenate(parts, axis=0)


def weight_gradient(field, delta, put):
    low = lax.broadcasted_iota(jnp.int32, (1, LANES), 1) < C
    turned = jnp.transpose(delta[:, :C]).astype(jnp.bfloat16)
    held = None
    for pair in range(PAIRS):
        got = matmul(turned, field.window(pair))
        first, last = got[:, :LANES], got[:, LANES:]
        block = 3 * (pair // 2)
        if pair % 2 == 0:
            put(block, first.astype(jnp.bfloat16))
            held = last
        else:
            first = jnp.concatenate([first[:, C:], first[:, :C]], axis=1)
            put(block + 1, jnp.where(low, held, first).astype(jnp.bfloat16))
            put(block + 2, jnp.where(low, first, last).astype(jnp.bfloat16))
    put(BLOCKS - 1, held.astype(jnp.bfloat16))


def upright(turned):
    return jnp.transpose(jnp.concatenate([turned, turned], axis=0))


def spread_plain(weight, plain):
    for pair in range(PAIRS):
        plain[pair, 3 * C :, :] = jnp.zeros((C, LANES), jnp.bfloat16)
    for at in range(0, TAPS, 2):
        taps = min(2, TAPS - at)
        stood = upright(weight[:, at * C : (at + taps) * C])
        for tap in range(at, at + taps):
            pair, c = tap // 3, tap % 3
            plain[pair, c * C : (c + 1) * C, :] = stood[(tap - at) * C : (tap - at + 1) * C]


def spread_flip(weight, flip):
    for pair in range(PAIRS):
        flip[pair, 3 * C :, :] = jnp.zeros((C, LANES), jnp.bfloat16)
    for tap in range(TAPS):
        pair, c = (TAPS - 1 - tap) // 3, (TAPS - 1 - tap) % 3
        flip[pair, c * C : (c + 1) * C, :] = twice(weight[:, tap * C : (tap + 1) * C])


def step_kernel(
    scenes, bricks, features_in, cotangent_in, first_weight_in, second_weight_in, send_in, gather_in,
    output_out, grad_input_out, grad_first_out, grad_second_out,
    output, grad_input, grad_first, grad_second, store_sems,
    features, cotangent, first_weight, second_weight, send_rows, gather_rows, load_sems,
    indices, columns, gather_hot, send_hot, pads, halo_out, halo_in, halo_send, halo_recv,
    first_plain, first_flip, second_plain, second_flip,
    even_in, odd_in, even_act, odd_act, even_delta, odd_delta, first_slope, word_sems, *reduction,
):
    pos = Position(scenes, bricks)
    peers = pos.near_peers()
    word = Word(pos, word_sems)
    loads = [
        pltpu.make_async_copy(source, target, load_sems.at[at])
        for at, (source, target) in enumerate((
            (send_in, send_rows), (features_in, features), (gather_in, gather_rows),
            (first_weight_in, first_weight), (second_weight_in, second_weight),
            (cotangent_in, cotangent),
        ))
    ]
    for load in loads:
        load.start()
    greet(peers)
    half = len(reduction) // 2
    first_sum = Reduction(pos, reduction[:half])
    second_sum = Reduction(pos, reduction[half:])
    halos = []
    stores = []

    def store(source, target):
        stores.append(pltpu.make_async_copy(source, target, store_sems.at[len(stores)]))
        stores[-1].start()

    def send_halo(values):
        at = len(halos)
        halo_out[at] = matmul(send_hot[...], values).astype(jnp.bfloat16)
        if at == 0:
            await_peers(peers)
        halos.append([
            remote(halo_out.at[at, pl.ds(64 * way, 64)], halo_in.at[at, pl.ds(64 * (1 - way), 64)],
                   halo_send.at[at, way], halo_recv.at[at, way], peer)
            for way, peer in enumerate((pos.down_id(), pos.up_id()))
        ])

    def gather_local(values):
        for c in range(3):
            for at in range(0, SLAB, 160):
                pads[c, at : at + 160] = matmul(gather_hot[c, at : at + 160, :VOX], values)

    def gather_halo(field):
        at = len(halos) - 1
        for copy in halos[at]:
            copy.wait_recv()
        rows = halo_in[at]
        field.fill(pads, gather_hot, rows)

    loads[0].wait()
    send_hot[...] = hot(as_columns(send_rows[...].astype(jnp.float32)), VOX)
    loads[1].wait()
    feature_rows = upright(features[...])
    send_halo(feature_rows)
    word.give(0)

    loads[2].wait()

    indices[...] = jnp.full(indices.shape, float(POOL), jnp.float32)
    indices[:, :CELLS] = jnp.broadcast_to(gather_rows[...].astype(jnp.float32), (EDGE, CELLS))
    for at in range(0, 1024, LANES):
        columns[pl.ds(at, LANES), :] = as_columns(indices[0:1, at : at + LANES])
    for c in range(3):
        taken = jnp.concatenate(
            [columns[pl.ds(SPAN * row + c, EDGE), :] for row in range(SPAN * SPAN)], axis=0
        )
        gather_hot[c] = hot(taken, POOL)
    gather_local(feature_rows)
    loads[3].wait()
    spread_plain(first_weight, first_plain)
    for one in (first_sum, second_sum):
        for block in (BLOCKS, BLOCKS + 1):
            one.put(block, jnp.zeros((C, LANES), jnp.bfloat16))

    field_in = Field(even_in, odd_in)
    field_act = Field(even_act, odd_act)
    field_delta = Field(even_delta, odd_delta)

    gather_halo(field_in)
    word.take(0)
    word.give(1)
    first_pre = field_in.conv(first_plain)
    sig = jax.nn.sigmoid(first_pre)
    first_act = (first_pre * sig).astype(jnp.bfloat16)
    send_halo(first_act)
    gather_local(first_act)
    first_slope[...] = sig * (1.0 + first_pre * (1.0 - sig))
    loads[4].wait()
    spread_plain(second_weight, second_plain)
    loads[5].wait()
    cot = upright(cotangent[...]).astype(jnp.float32)
    gather_halo(field_act)
    word.take(1)
    word.give(2)
    second_pre = field_act.conv(second_plain)
    sig = jax.nn.sigmoid(second_pre)
    slope = sig * (1.0 + second_pre * (1.0 - sig))
    second_delta32 = cot * slope
    second_delta = second_delta32.astype(jnp.bfloat16)
    send_halo(second_delta)
    weight_gradient(field_act, second_delta32, second_sum.put)
    second_sum.start_scene()
    gather_local(second_delta)
    spread_flip(second_weight, second_flip)
    output[...] = jnp.transpose(second_pre * sig)[:C].astype(jnp.bfloat16)
    store(output, output_out)
    gather_halo(field_delta)
    word.take(2)
    first_delta32 = field_delta.conv(second_flip) * first_slope[...]
    weight_gradient(field_in, first_delta32, first_sum.put)
    first_sum.start_scene()
    first_delta = first_delta32.astype(jnp.bfloat16)
    send_halo(first_delta)
    spread_flip(first_weight, first_flip)
    gather_local(first_delta)
    second_sum.start_row()
    gather_halo(field_delta)
    second_sum.start_col()
    first_sum.start_row()
    grad_input[...] = jnp.transpose(field_delta.conv(first_flip))[:C].astype(jnp.bfloat16)
    store(grad_input, grad_input_out)
    first_sum.start_col()
    second_sum.start_row_back()
    second_sum.start_scene_back()
    first_sum.start_row_back()
    first_sum.start_scene_back()
    scale = float(scenes * bricks * VOX) ** (-0.5)
    second_sum.finish(grad_second, scale)
    store(grad_second, grad_second_out)
    first_sum.finish(grad_first, scale)
    store(grad_first, grad_first_out)
    for copy in stores:
        copy.wait()
    for pair in halos:
        for copy in pair:
            copy.wait_send()


def hand_over(*refs):
    count = 4
    sources, targets, held = refs[:count], refs[count : 2 * count], refs[2 * count : 3 * count]
    load_sems, store_sems = refs[3 * count :]
    loads = [pltpu.make_async_copy(sources[at], held[at], load_sems.at[at]) for at in range(count)]
    stores = [pltpu.make_async_copy(held[at], targets[at], store_sems.at[at]) for at in range(count)]
    for load in loads:
        load.start()
    for load, store in zip(loads, stores):
        load.wait()
        store.start()
    for store in stores:
        store.wait()


def shards(features, cotangent, first_weight, second_weight, send_rows, gather_rows):
    scenes, bricks = lax.axis_size("scene"), lax.axis_size("brick")
    rows, cols = brick_grid(bricks)
    field = jax.ShapeDtypeStruct((C, VOX), jnp.bfloat16)
    grad = jax.ShapeDtypeStruct((C, TAPS * C), jnp.float32)
    operands = [features[0].T, cotangent[0].T, first_weight.T, second_weight.T, send_rows, gather_rows]
    even = pltpu.VMEM((SPAN, SPAN * EDGE, DEEP), jnp.bfloat16)
    odd = pltpu.VMEM((SPAN, VOX // EDGE, DEEP), jnp.bfloat16)
    spread = pltpu.VMEM((PAIRS, DEEP, LANES), jnp.bfloat16)
    halo = pltpu.VMEM((EXCHANGES, LANES, LANES), jnp.bfloat16)
    results = [pltpu.VMEM(one.shape, one.dtype) for one in (field, field, grad, grad)]
    results.append(pltpu.SemaphoreType.DMA((4,)))
    scratch = results + [pltpu.VMEM(one.shape, one.dtype) for one in operands] + [
        pltpu.SemaphoreType.DMA((len(operands),)),
        pltpu.VMEM((EDGE, 1024), jnp.float32),
        pltpu.VMEM((1024, LANES), jnp.float32),
        pltpu.VMEM((3, SLAB, POOL), jnp.bfloat16),
        pltpu.VMEM((LANES, VOX), jnp.bfloat16),
        pltpu.VMEM((3, SLAB, LANES), jnp.float32),
        halo,
        halo,
        pltpu.SemaphoreType.DMA((EXCHANGES, 2)),
        pltpu.SemaphoreType.DMA((EXCHANGES, 2)),
        spread, spread, spread, spread,
        even, odd, even, odd, even, odd,
        pltpu.VMEM((VOX, LANES), jnp.float32),
        pltpu.SemaphoreType.REGULAR((5,)),
    ]
    out, grad_in, grad_first, grad_second = pl.pallas_call(
        functools.partial(step_kernel, scenes, bricks),
        out_shape=(field, field, grad, grad),
        in_specs=[pl.BlockSpec(memory_space=pltpu.HBM)] * 6,
        out_specs=[pl.BlockSpec(memory_space=pltpu.HBM)] * 4,
        scratch_shapes=scratch + Reduction.scratch(scenes, rows, cols) * 2,
        compiler_params=pltpu.CompilerParams(
            collective_id=0, has_side_effects=True, vmem_limit_bytes=62 * 1024 * 1024
        ),
    )(*operands)
    out, grad_in, grad_first, grad_second = pl.pallas_call(
        hand_over,
        out_shape=(field, field, grad, grad),
        in_specs=[pl.BlockSpec(memory_space=pltpu.HBM)] * 4,
        out_specs=[pl.BlockSpec(memory_space=pltpu.HBM)] * 4,
        scratch_shapes=results[:4] + [pltpu.SemaphoreType.DMA((4,))] * 2,
        compiler_params=pltpu.CompilerParams(vmem_limit_bytes=62 * 1024 * 1024),
    )(out, grad_in, grad_first, grad_second)
    return out.T[None], grad_in.T[None], grad_first.T, grad_second.T


def solution(mesh):
    in_specs = (
        P("scene", "brick", None),
        P("scene", "brick", None),
        P(),
        P(),
        P("scene", "brick"),
        P("scene", "brick"),
    )
    out_specs = (P("scene", "brick", None), P("scene", "brick", None), P(), P())
    return jax.shard_map(shards, mesh=mesh, in_specs=in_specs, out_specs=out_specs, check_vma=False)
```

```python
import functools

import jax
import jax.numpy as jnp
from jax import lax
from jax.experimental import pallas as pl
from jax.experimental.pallas import tpu as pltpu
from jax.sharding import PartitionSpec as P

EDGE = 8
VOX = 512
C = 64
TAPS = 27
LANES = 128
MESH = pl.DeviceIdType.MESH
BLOCKS = 14
SPAN = EDGE + 2
CELLS = SPAN**3
SLAB = SPAN * SPAN * EDGE
POOL = VOX + LANES
PAIRS = 9
DEEP = 256
EXCHANGES = 4


def brick_grid(count):
    for rows in (8, 4, 2):
        if count % rows == 0 and count // rows > 1:
            return rows, count // rows
    return 1, count


def far_first(count):
    return sorted(range(1, count), key=lambda step: (-min(step, count - step), step))


class Position:
    def __init__(self, scenes, bricks):
        self.scenes = scenes
        self.bricks = bricks
        self.rows, self.cols = brick_grid(bricks)
        self.scene = lax.axis_index("scene")
        self.brick = lax.axis_index("brick")
        self.row = self.brick // self.cols
        self.col = lax.rem(self.brick, self.cols)

    def scene_peer(self, step):
        return lax.rem(self.scene + step, self.scenes)

    def row_peer(self, step):
        return lax.rem(self.row + step, self.rows)

    def col_peer(self, step):
        return lax.rem(self.col + step, self.cols)

    def scene_id(self, step):
        return (self.scene_peer(step), self.brick)

    def row_id(self, step):
        return (self.scene, self.row_peer(step) * self.cols + self.col)

    def col_id(self, step):
        return (self.scene, self.row * self.cols + self.col_peer(step))

    def down_id(self):
        return (self.scene, lax.rem(self.brick + self.bricks - 1, self.bricks))

    def up_id(self):
        return (self.scene, lax.rem(self.brick + 1, self.bricks))

    def near_peers(self):
        peers = [self.down_id(), self.up_id()] + self.row_pair(1) + self.col_pair(1)
        return peers + [self.scene_id(k) for k in far_first(self.scenes)]

    def row_pair(self, step):
        return [self.row_id(step), self.row_id(self.rows - step)]

    def col_pair(self, step):
        return [self.col_id(step), self.col_id(self.cols - step)]


class Word:
    def __init__(self, pos, sems):
        self.rounds = [
            [(sems.at[0], pos.col_pair(1)), (sems.at[1], pos.row_pair(1))],
            [(sems.at[2], pos.col_pair(2)), (sems.at[3], pos.row_pair(2))],
            [(sems.at[4], pos.col_pair(4))],
        ]

    def give(self, at):
        for sem, peers in self.rounds[at]:
            for peer in peers:
                pl.semaphore_signal(sem, inc=1, device_id=peer, device_id_type=MESH)

    def take(self, at):
        for sem, peers in self.rounds[at]:
            pl.semaphore_wait(sem, len(peers))


def greet(peers):
    barrier = pltpu.get_barrier_semaphore()
    for peer in peers:
        pl.semaphore_signal(barrier, inc=1, device_id=peer, device_id_type=MESH)


def await_peers(peers):
    pl.semaphore_wait(pltpu.get_barrier_semaphore(), len(peers))


def remote(src, dst, send_sem, recv_sem, peer):
    copy = pltpu.make_async_remote_copy(
        src_ref=src, dst_ref=dst, send_sem=send_sem, recv_sem=recv_sem,
        device_id=peer, device_id_type=MESH,
    )
    copy.start()
    return copy


class Reduction:
    def __init__(self, pos, refs):
        self.pos = pos
        (self.send_scene, self.recv_scene, self.send_row, self.recv_row,
         self.slots, self.full, *sems) = refs
        self.sems = [(sems[2 * i], sems[2 * i + 1]) for i in range(5)]
        self.started = []

    @staticmethod
    def scratch(scenes, rows, cols):
        piece = 1024 // scenes
        small = piece // rows
        counts = (scenes, rows, cols, rows, scenes)
        sems = []
        for count in counts:
            sems += [pltpu.SemaphoreType.DMA((count - 1,))] * 2
        return [
            pltpu.VMEM((scenes, piece, LANES), jnp.bfloat16),
            pltpu.VMEM((scenes - 1, piece, LANES), jnp.bfloat16),
            pltpu.VMEM((rows, small, LANES), jnp.bfloat16),
            pltpu.VMEM((rows - 1, small, LANES), jnp.bfloat16),
            pltpu.VMEM((cols, small, LANES), jnp.bfloat16),
            pltpu.VMEM((scenes, rows, small, LANES), jnp.bfloat16),
        ] + sems

    def put(self, block, values):
        piece = self.send_scene.shape[1]
        rows = values.shape[0]
        start = block * rows
        for at in range(start, start + rows, min(rows, piece)):
            count = min(rows, piece)
            self.send_scene[at // piece, pl.ds(at % piece, count), :] = values[
                at - start : at - start + count
            ]

    def send(self, which, src, dst, peers):
        sems = self.sems[which]
        self.current = [
            remote(src[step - 1], dst[step - 1], sems[0].at[step - 1], sems[1].at[step - 1],
                   peers[step - 1])
            for step in far_first(len(peers) + 1)
        ]
        self.started += self.current

    def arrive(self):
        for copy in self.current:
            copy.wait_recv()

    def start_scene(self):
        pos = self.pos
        n = pos.scenes
        self.send(0, [self.send_scene.at[pos.scene_peer(k)] for k in range(1, n)],
                  [self.recv_scene.at[k - 1] for k in range(1, n)],
                  [pos.scene_id(k) for k in range(1, n)])

    def start_row(self):
        self.arrive()
        pos = self.pos
        n = pos.rows
        total = self.send_scene[pos.scene].astype(jnp.float32)
        for k in range(pos.scenes - 1):
            total = total + self.recv_scene[k].astype(jnp.float32)
        self.send_row[...] = total.astype(jnp.bfloat16).reshape(self.send_row.shape)
        self.send(1, [self.send_row.at[pos.row_peer(k)] for k in range(1, n)],
                  [self.recv_row.at[k - 1] for k in range(1, n)],
                  [pos.row_id(k) for k in range(1, n)])

    def start_col(self):
        self.arrive()
        pos = self.pos
        n = pos.cols
        total = self.send_row[pos.row].astype(jnp.float32)
        for k in range(pos.rows - 1):
            total = total + self.recv_row[k].astype(jnp.float32)
        self.slots[pos.col] = total.astype(jnp.bfloat16)
        own = self.slots.at[pos.col]
        self.send(2, [own] * (n - 1), [own] * (n - 1), [pos.col_id(k) for k in range(1, n)])

    def start_row_back(self):
        self.arrive()
        pos = self.pos
        n = pos.rows
        total = self.slots[0].astype(jnp.float32)
        for k in range(1, pos.cols):
            total = total + self.slots[k].astype(jnp.float32)
        self.full[pos.scene, pos.row] = total.astype(jnp.bfloat16)
        own = self.full.at[pos.scene, pos.row]
        self.send(3, [own] * (n - 1), [own] * (n - 1), [pos.row_id(k) for k in range(1, n)])

    def start_scene_back(self):
        self.arrive()
        pos = self.pos
        n = pos.scenes
        own = self.full.at[pos.scene]
        self.send(4, [own] * (n - 1), [own] * (n - 1), [pos.scene_id(k) for k in range(1, n)])

    def finish(self, out, scale):
        self.arrive()
        everything = self.full[...].reshape(1024, LANES)
        for block in range(BLOCKS):
            lanes = min(LANES, TAPS * C - block * LANES)
            piece = everything[block * C : (block + 1) * C].astype(jnp.float32) * scale
            out[:, block * LANES : block * LANES + lanes] = piece[:, :lanes]
        for copy in self.started:
            copy.wait_send()


def hot(columns, width):
    lane = lax.broadcasted_iota(jnp.int32, (1, LANES), 1).astype(jnp.float32)
    parts = [
        jnp.where(columns == lane + float(at), 1.0, 0.0).astype(jnp.bfloat16)
        for at in range(0, width, LANES)
    ]
    return jnp.concatenate(parts, axis=1)


def as_columns(row):
    return jnp.transpose(jnp.broadcast_to(row, (LANES, LANES)))


def twice(values):
    return jnp.concatenate([values, values], axis=1)


def matmul(left, right):
    return jnp.dot(left, right, preferred_element_type=jnp.float32)


class Field:
    def __init__(self, even, odd):
        self.even = even
        self.odd = odd

    def window(self, pair):
        a, b = pair // 3, pair % 3
        if b == 1:
            rows = self.odd[a : a + EDGE]
        else:
            rows = self.even[a : a + EDGE, EDGE * b : EDGE * b + VOX // EDGE]
        return rows.reshape(VOX, DEEP)

    def fill(self, pads, halo_hot, rows):
        low = lax.broadcasted_iota(jnp.int32, (1, LANES), 1) < C
        for plane in range(0, SPAN, 2):
            span = slice(plane * SPAN * EDGE, (plane + 2) * SPAN * EDGE)
            cells = [pads[c, span] + matmul(halo_hot[c, span, VOX:], rows) for c in range(3)]
            for lane, values in ((0, jnp.where(low, cells[0], cells[1])), (LANES, cells[2])):
                for half in range(2):
                    part = values[half * SPAN * EDGE : (half + 1) * SPAN * EDGE]
                    self.even[plane + half, :, lane : lane + LANES] = part.astype(jnp.bfloat16)
                    self.odd[plane + half, :, lane : lane + LANES] = part[
                        EDGE : EDGE + VOX // EDGE
                    ].astype(jnp.bfloat16)

    def conv(self, weight):
        rows = VOX // 2
        parts = []
        for at in range(2):
            total = matmul(self.window(0)[at * rows : (at + 1) * rows], weight[0])
            for pair in range(1, PAIRS):
                total = total + matmul(self.window(pair)[at * rows : (at + 1) * rows], weight[pair])
            parts.append(total)
        return jnp.concatenate(parts, axis=0)


def weight_gradient(field, delta, put):
    low = lax.broadcasted_iota(jnp.int32, (1, LANES), 1) < C
    turned = jnp.transpose(delta[:, :C]).astype(jnp.bfloat16)
    held = None
    for pair in range(PAIRS):
        got = matmul(turned, field.window(pair))
        first, last = got[:, :LANES], got[:, LANES:]
        block = 3 * (pair // 2)
        if pair % 2 == 0:
            put(block, first.astype(jnp.bfloat16))
            held = last
        else:
            first = jnp.concatenate([first[:, C:], first[:, :C]], axis=1)
            put(block + 1, jnp.where(low, held, first).astype(jnp.bfloat16))
            put(block + 2, jnp.where(low, first, last).astype(jnp.bfloat16))
    put(BLOCKS - 1, held.astype(jnp.bfloat16))


def upright(turned):
    return jnp.transpose(jnp.concatenate([turned, turned], axis=0))


def spread_plain(weight, plain):
    for pair in range(PAIRS):
        plain[pair, 3 * C :, :] = jnp.zeros((C, LANES), jnp.bfloat16)
    for at in range(0, TAPS, 2):
        taps = min(2, TAPS - at)
        stood = upright(weight[:, at * C : (at + taps) * C])
        for tap in range(at, at + taps):
            pair, c = tap // 3, tap % 3
            plain[pair, c * C : (c + 1) * C, :] = stood[(tap - at) * C : (tap - at + 1) * C]


def spread_flip(weight, flip):
    for pair in range(PAIRS):
        flip[pair, 3 * C :, :] = jnp.zeros((C, LANES), jnp.bfloat16)
    for tap in range(TAPS):
        pair, c = (TAPS - 1 - tap) // 3, (TAPS - 1 - tap) % 3
        flip[pair, c * C : (c + 1) * C, :] = twice(weight[:, tap * C : (tap + 1) * C])


def step_kernel(
    scenes, bricks, features_in, cotangent_in, first_weight_in, second_weight_in, send_in, gather_in,
    output_out, grad_input_out, grad_first_out, grad_second_out,
    output, grad_input, grad_first, grad_second, store_sems,
    features, cotangent, first_weight, second_weight, send_rows, gather_rows, load_sems,
    indices, columns, gather_hot, send_hot, pads, halo_out, halo_in, halo_send, halo_recv,
    first_plain, first_flip, second_plain, second_flip,
    even_in, odd_in, even_act, odd_act, even_delta, odd_delta, first_slope, word_sems, *reduction,
):
    pos = Position(scenes, bricks)
    peers = pos.near_peers()
    word = Word(pos, word_sems)
    loads = [
        pltpu.make_async_copy(source, target, load_sems.at[at])
        for at, (source, target) in enumerate((
            (send_in, send_rows), (features_in, features), (gather_in, gather_rows),
            (first_weight_in, first_weight), (second_weight_in, second_weight),
            (cotangent_in, cotangent),
        ))
    ]
    for load in loads:
        load.start()
    greet(peers)
    half = len(reduction) // 2
    first_sum = Reduction(pos, reduction[:half])
    second_sum = Reduction(pos, reduction[half:])
    halos = []
    stores = []

    def store(source, target):
        stores.append(pltpu.make_async_copy(source, target, store_sems.at[len(stores)]))
        stores[-1].start()

    def send_halo(values):
        at = len(halos)
        halo_out[at] = matmul(send_hot[...], values).astype(jnp.bfloat16)
        if at == 0:
            await_peers(peers)
        halos.append([
            remote(halo_out.at[at, pl.ds(64 * way, 64)], halo_in.at[at, pl.ds(64 * (1 - way), 64)],
                   halo_send.at[at, way], halo_recv.at[at, way], peer)
            for way, peer in enumerate((pos.down_id(), pos.up_id()))
        ])

    def gather_local(values):
        for c in range(3):
            for at in range(0, SLAB, 160):
                pads[c, at : at + 160] = matmul(gather_hot[c, at : at + 160, :VOX], values)

    def gather_halo(field):
        at = len(halos) - 1
        for copy in halos[at]:
            copy.wait_recv()
        rows = halo_in[at]
        field.fill(pads, gather_hot, rows)

    loads[0].wait()
    send_hot[...] = hot(as_columns(send_rows[...].astype(jnp.float32)), VOX)
    loads[1].wait()
    feature_rows = upright(features[...])
    send_halo(feature_rows)
    word.give(0)

    loads[2].wait()

    indices[...] = jnp.full(indices.shape, float(POOL), jnp.float32)
    indices[:, :CELLS] = jnp.broadcast_to(gather_rows[...].astype(jnp.float32), (EDGE, CELLS))
    for at in range(0, 1024, LANES):
        columns[pl.ds(at, LANES), :] = as_columns(indices[0:1, at : at + LANES])
    for c in range(3):
        taken = jnp.concatenate(
            [columns[pl.ds(SPAN * row + c, EDGE), :] for row in range(SPAN * SPAN)], axis=0
        )
        gather_hot[c] = hot(taken, POOL)
    gather_local(feature_rows)
    loads[3].wait()
    spread_plain(first_weight, first_plain)
    for one in (first_sum, second_sum):
        for block in (BLOCKS, BLOCKS + 1):
            one.put(block, jnp.zeros((C, LANES), jnp.bfloat16))

    field_in = Field(even_in, odd_in)
    field_act = Field(even_act, odd_act)
    field_delta = Field(even_delta, odd_delta)

    gather_halo(field_in)
    word.take(0)
    word.give(1)
    first_pre = field_in.conv(first_plain)
    sig = jax.nn.sigmoid(first_pre)
    first_act = (first_pre * sig).astype(jnp.bfloat16)
    send_halo(first_act)
    gather_local(first_act)
    first_slope[...] = sig * (1.0 + first_pre * (1.0 - sig))
    loads[4].wait()
    spread_plain(second_weight, second_plain)
    loads[5].wait()
    cot = upright(cotangent[...]).astype(jnp.float32)
    gather_halo(field_act)
    word.take(1)
    word.give(2)
    second_pre = field_act.conv(second_plain)
    sig = jax.nn.sigmoid(second_pre)
    slope = sig * (1.0 + second_pre * (1.0 - sig))
    second_delta32 = cot * slope
    second_delta = second_delta32.astype(jnp.bfloat16)
    send_halo(second_delta)
    weight_gradient(field_act, second_delta32, second_sum.put)
    second_sum.start_scene()
    gather_local(second_delta)
    spread_flip(second_weight, second_flip)
    output[...] = jnp.transpose(second_pre * sig)[:C].astype(jnp.bfloat16)
    store(output, output_out)
    gather_halo(field_delta)
    word.take(2)
    first_delta32 = field_delta.conv(second_flip) * first_slope[...]
    weight_gradient(field_in, first_delta32, first_sum.put)
    first_sum.start_scene()
    first_delta = first_delta32.astype(jnp.bfloat16)
    send_halo(first_delta)
    spread_flip(first_weight, first_flip)
    gather_local(first_delta)
    second_sum.start_row()
    gather_halo(field_delta)
    second_sum.start_col()
    first_sum.start_row()
    grad_input[...] = jnp.transpose(field_delta.conv(first_flip))[:C].astype(jnp.bfloat16)
    store(grad_input, grad_input_out)
    first_sum.start_col()
    second_sum.start_row_back()
    second_sum.start_scene_back()
    first_sum.start_row_back()
    first_sum.start_scene_back()
    scale = float(scenes * bricks * VOX) ** (-0.5)
    second_sum.finish(grad_second, scale)
    store(grad_second, grad_second_out)
    first_sum.finish(grad_first, scale)
    store(grad_first, grad_first_out)
    for copy in stores:
        copy.wait()
    for pair in halos:
        for copy in pair:
            copy.wait_send()


def hand_over(*refs):
    sources, targets, held = refs[:4], refs[4:8], refs[8:12]
    load_sems, store_sems = refs[12:]
    loads, stores = [], []
    for at in (2, 3, 0, 1):
        rows = held[at].shape[0] // 4 if at > 1 else held[at].shape[0]
        for start in range(0, held[at].shape[0], rows):
            part = pl.ds(start, rows)
            sem = len(loads)
            loads.append(pltpu.make_async_copy(
                sources[at].at[part], held[at].at[part], load_sems.at[sem]))
            stores.append(pltpu.make_async_copy(
                held[at].at[part], targets[at].at[part], store_sems.at[sem]))
            loads[-1].start()
    for load, store in zip(loads, stores):
        load.wait()
        store.start()
    for store in stores:
        store.wait()


def shards(features, cotangent, first_weight, second_weight, send_rows, gather_rows):
    scenes, bricks = lax.axis_size("scene"), lax.axis_size("brick")
    rows, cols = brick_grid(bricks)
    field = jax.ShapeDtypeStruct((C, VOX), jnp.bfloat16)
    grad = jax.ShapeDtypeStruct((C, TAPS * C), jnp.float32)
    operands = [features[0].T, cotangent[0].T, first_weight.T, second_weight.T, send_rows, gather_rows]
    even = pltpu.VMEM((SPAN, SPAN * EDGE, DEEP), jnp.bfloat16)
    odd = pltpu.VMEM((SPAN, VOX // EDGE, DEEP), jnp.bfloat16)
    spread = pltpu.VMEM((PAIRS, DEEP, LANES), jnp.bfloat16)
    halo = pltpu.VMEM((EXCHANGES, LANES, LANES), jnp.bfloat16)
    results = [pltpu.VMEM(one.shape, one.dtype) for one in (field, field, grad, grad)]
    results.append(pltpu.SemaphoreType.DMA((4,)))
    scratch = results + [pltpu.VMEM(one.shape, one.dtype) for one in operands] + [
        pltpu.SemaphoreType.DMA((len(operands),)),
        pltpu.VMEM((EDGE, 1024), jnp.float32),
        pltpu.VMEM((1024, LANES), jnp.float32),
        pltpu.VMEM((3, SLAB, POOL), jnp.bfloat16),
        pltpu.VMEM((LANES, VOX), jnp.bfloat16),
        pltpu.VMEM((3, SLAB, LANES), jnp.float32),
        halo,
        halo,
        pltpu.SemaphoreType.DMA((EXCHANGES, 2)),
        pltpu.SemaphoreType.DMA((EXCHANGES, 2)),
        spread, spread, spread, spread,
        even, odd, even, odd, even, odd,
        pltpu.VMEM((VOX, LANES), jnp.float32),
        pltpu.SemaphoreType.REGULAR((5,)),
    ]
    out, grad_in, grad_first, grad_second = pl.pallas_call(
        functools.partial(step_kernel, scenes, bricks),
        out_shape=(field, field, grad, grad),
        in_specs=[pl.BlockSpec(memory_space=pltpu.HBM)] * 6,
        out_specs=[pl.BlockSpec(memory_space=pltpu.HBM)] * 4,
        scratch_shapes=scratch + Reduction.scratch(scenes, rows, cols) * 2,
        compiler_params=pltpu.CompilerParams(
            collective_id=0, has_side_effects=True, vmem_limit_bytes=62 * 1024 * 1024
        ),
    )(*operands)
    out, grad_in, grad_first, grad_second = pl.pallas_call(
        hand_over,
        out_shape=(field, field, grad, grad),
        in_specs=[pl.BlockSpec(memory_space=pltpu.HBM)] * 4,
        out_specs=[pl.BlockSpec(memory_space=pltpu.HBM)] * 4,
        scratch_shapes=results[:4] + [pltpu.SemaphoreType.DMA((10,))] * 2,
        compiler_params=pltpu.CompilerParams(vmem_limit_bytes=62 * 1024 * 1024),
    )(out, grad_in, grad_first, grad_second)
    return out.T[None], grad_in.T[None], grad_first.T, grad_second.T


def solution(mesh):
    in_specs = (
        P("scene", "brick", None),
        P("scene", "brick", None),
        P(),
        P(),
        P("scene", "brick"),
        P("scene", "brick"),
    )
    out_specs = (P("scene", "brick", None), P("scene", "brick", None), P(), P())
    return jax.shard_map(shards, mesh=mesh, in_specs=in_specs, out_specs=out_specs, check_vma=False)
```
